256 devices in a mesh: section: 4 (over y), seq: 16 (over z, core), mp: 4 (over x).
Axes of the slice: x: 4, y: 4, z: 8, core: 2. Of those that a mesh axis runs over, the one named last changes fastest.
Arguments:
- x_in: bfloat16 [4, 4096, 4096], P('section', 'seq', 'mp'), may hold values from -17 to 17
- cotangent: bfloat16 [4, 4096, 4096], P('section', 'seq', 'mp'), may hold values from -8 to 8
- tok_weight: float32 [4, 4096], P('section', 'seq'), may hold values from -4 to 4
- neighbours: int32 [4, 64, 2], P('section', 'seq'), may hold values from 0 to 63, as said below
- w_query: bfloat16 [4, 4096, 2048], P('section', None, 'mp'), may hold values from -0.09375 to 0.09375
- w_key: bfloat16 [4, 896, 2048], P('section', None, 'mp'), may hold values from -0.1875 to 0.1875
- w_value: bfloat16 [4, 896, 2048], P('section', None, 'mp'), may hold values from -0.1875 to 0.1875
- w_out: bfloat16 [4, 2048, 4096], P('section', 'mp'), may hold values from -0.5 to 0.5
- encodings: bfloat16 [4, 64, 128, 896], P('section', 'seq', 'mp'), may hold values from -6.8 to 6.8
Outputs:
- next_input: bfloat16 [4, 4096, 4096], P('section', 'seq', 'mp')
- prev_grad: bfloat16 [4, 4096, 4096], P('section', 'seq', 'mp')
- grad_query: bfloat16 [4, 4096, 2048], P('section', 'seq', 'mp')
- grad_key: bfloat16 [4, 896, 2048], P('section', 'seq', 'mp')
- grad_value: bfloat16 [4, 896, 2048], P('section', 'seq', 'mp')
- grad_out: bfloat16 [4, 2048, 4096], P('section', 'mp', 'seq')
- grad_enc: bfloat16 [4, 64, 128, 896], P('section', 'seq', 'mp')
The draws below stay inside these ranges and needn't reach their ends.
Inputs may be any that keep to these rules, and one draw needn't show every extreme that they name: `neighbours`: each span names 2 different blocks; block b belongs to the owner b // 4. Of the 8 names made by the spans of one index of seq, at most 2 fall on the blocks of any one owner, and some owner receives exactly 2 of them.
All inputs are finite; a program needn't handle non-finite values.
Results may differ from the reference program's by a relative error of at most 0.024.
The reference program's roundings to bfloat16 on the way count: a program that leaves them out, or rounds other values in their place, can miss the bound.
Values may be sent and summed in bfloat16 or wider, within the bound.
No kernel may reach another device: no remote copies, remote signals or barrier semaphores. Data moves between devices by JAX's collectives and lax.ppermute only.
A program may use at most 128 MiB of HBM per device.

```python
import math
import jax
import jax.numpy as jnp
import numpy as np
from jax import lax

D = 4096
HEADS = 16
HD = 128
DE = 896
CL = 64
NEIGH = 2
NBLEN = 128
TOK_DEV = 256
CH_DEV = 4
ENC_DEV = 4
CAP = 2
HEAD_GROUP = 4
SECTIONS = 4
TOKENS = 4096
SPANS = 64
ENC_BLOCKS = 64
N_MP = 4


def draw_x_in(key, part):
    key = jax.random.fold_in(key, 11)
    base_key = jax.random.fold_in(key, 0)
    draw_shape = (SECTIONS, TOKENS, D)
    values = jnp.clip(jax.random.normal(base_key, draw_shape, jnp.float32), -6.0, 6.0)
    return values.astype(jnp.bfloat16)


def draw_encodings(key, part):
    key = jax.random.fold_in(key, 23)
    base_key = jax.random.fold_in(key, 0)
    draw_shape = (SECTIONS, ENC_BLOCKS, NBLEN, DE)
    values = jnp.clip(jax.random.normal(base_key, draw_shape, jnp.float32), -6.0, 6.0)
    return values.astype(jnp.bfloat16)


def draw_neighbours(key, part):
    key = jax.random.fold_in(key, 37)
    owners = ENC_BLOCKS // ENC_DEV
    use_count = CH_DEV * NEIGH
    counts = [0] * owners
    counts[0] = CAP
    remaining = use_count - CAP
    base_count = remaining // (owners - 1)
    extra_count = remaining % (owners - 1)
    for owner_rank in range(1, owners):
        counts[owner_rank] = base_count + (1 if owner_rank - 1 < extra_count else 0)
    rank_table = np.repeat(np.arange(owners), counts).astype(np.int32)
    ordinal_table = np.concatenate([np.arange(amount) for amount in counts]).astype(np.int32)

    def local_order(local_key):
        return jax.random.permutation(local_key, ENC_DEV)

    def one_block(block_key):
        owner_key, local_key, shuffle_key = jax.random.split(block_key, 3)
        owner_perm = jax.random.permutation(owner_key, owners)
        local_perm = jax.vmap(local_order)(jax.random.split(local_key, owners))
        owner_of_use = owner_perm[rank_table]
        local_of_use = local_perm[rank_table, ordinal_table]
        block_ids = owner_of_use * ENC_DEV + local_of_use
        block_ids = block_ids[jax.random.permutation(shuffle_key, use_count)]
        return block_ids.reshape(CH_DEV, NEIGH)
    blocks_drawn = jax.vmap(one_block)(jax.random.split(key, SECTIONS * owners))
    return blocks_drawn.reshape(SECTIONS, SPANS, NEIGH).astype(jnp.int32)


def with_spikes(entries, key, source, target, parts, factor):
    def block_of(dim):
        return (jnp.arange(entries.shape[dim]) // (entries.shape[dim] // parts)).reshape((-1,) + (1,) * (entries.ndim - 1 - dim))

    near = jax.random.permutation(key, parts)[block_of(target)]
    other_side = (block_of(target) + parts // 2) % parts
    return jnp.where((block_of(source) == near) | (block_of(source) == other_side), factor * entries, entries)


def block_levels(key, shape, pieces, least, largest):
    factor_of, own = 1.0, jax.random.fold_in(key, 6)
    for dim, blocks in pieces:
        draws = jnp.exp(jax.random.uniform(jax.random.fold_in(own, dim), (blocks,), jnp.float32, least / len(pieces), largest / len(pieces)))
        factor_of = factor_of * jnp.repeat(draws, shape[dim] // blocks).reshape([-1 if axis == dim else 1 for axis in range(len(shape))])
    return factor_of


def normal_values(own_key, extent, scale, bound, cuts=(), kind=jnp.bfloat16):
    result = jax.random.normal(own_key, extent, jnp.float32) * scale
    if len(cuts) > 0:
        result = block_levels(own_key, extent, cuts, -0.22, 0.18) * result
    return jnp.clip(result, min=-bound, max=bound).astype(kind)


def bell_draw_with(rng, extent, scale, reach, pieces, heavy, held_as=jnp.bfloat16):
    drawn = scale * jax.random.normal(rng, extent, jnp.float32)
    if pieces:
        drawn = drawn * block_levels(rng, extent, pieces, -0.22, 0.18)
    return jnp.clip(with_spikes(drawn, jax.random.fold_in(rng, 3), *heavy), -reach, reach).astype(held_as)


def setup_inputs(seed: int = 0) -> dict:
    splits = jax.random.split(jax.random.key(seed), 10)
    return {
        "x_in": draw_x_in(jax.random.fold_in(splits[9], 71), 0),
        "cotangent": bell_draw_with(splits[1], (SECTIONS, TOKENS, D), 1.0, 8.0, ((0, 4), (1, 16), (2, 4)), (1, 2, 16, 2.0)),
        "tok_weight": normal_values(splits[2], (SECTIONS, TOKENS), 1.0, 4.0, ((0, 4), (1, 16)), jnp.float32),
        "neighbours": draw_neighbours(jax.random.fold_in(splits[9], 71), 0),
        "w_query": normal_values(splits[4], (SECTIONS, D, HEADS * HD), D ** -0.5, 0.09375, ((0, 4), (2, 4))),
        "w_key": normal_values(splits[5], (SECTIONS, DE, HEADS * HD), DE ** -0.5, 0.1875, ((0, 4), (2, 4))),
        "w_value": normal_values(splits[6], (SECTIONS, DE, HEADS * HD), DE ** -0.5, 0.1875, ((0, 4), (2, 4))),
        "w_out": normal_values(splits[7], (SECTIONS, HEADS * HD, D), HD ** -0.5, 0.5, ((0, 4), (1, 4))),
        "encodings": draw_encodings(jax.random.fold_in(splits[9], 71), 0),
    }


def rounded(value):
    return lax.optimization_barrier(value.astype(jnp.bfloat16)).astype(jnp.float32)

def group_sum(first_factor, second_factor):
    group_width = HEAD_GROUP * HD
    running = jnp.zeros((first_factor.shape[0], second_factor.shape[1]), jnp.float32)
    for group_index in range(N_MP):
        column_start = group_index * group_width
        piece = jnp.dot(first_factor[:, column_start:column_start + group_width], second_factor[column_start:column_start + group_width, :], preferred_element_type=jnp.float32)
        running = running + rounded(piece)
    return running

def block_sum(first_factor, second_factor, row_block):
    running = jnp.zeros((first_factor.shape[1], second_factor.shape[1]), jnp.float32)
    for block_index in range(first_factor.shape[0] // row_block):
        row_start = block_index * row_block
        piece = jnp.dot(first_factor[row_start:row_start + row_block].T, second_factor[row_start:row_start + row_block], preferred_element_type=jnp.float32)
        running = running + rounded(piece)
    return running.astype(jnp.bfloat16)

def one_section(x_rows, cot_rows, token_scale, block_ids, query_proj, key_proj, value_proj, out_proj, enc_blocks):
    score_scale = 1.0 / math.sqrt(HD)
    total_cols = HEADS * HD
    query_rows = jnp.dot(x_rows, query_proj, preferred_element_type=jnp.float32).astype(jnp.bfloat16)
    flat_enc = enc_blocks.reshape(ENC_BLOCKS * NBLEN, DE)
    key_blocks = jnp.dot(flat_enc, key_proj, preferred_element_type=jnp.float32).astype(jnp.bfloat16)
    value_blocks = jnp.dot(flat_enc, value_proj, preferred_element_type=jnp.float32).astype(jnp.bfloat16)
    key_blocks = key_blocks.reshape(ENC_BLOCKS, NBLEN, total_cols)
    value_blocks = value_blocks.reshape(ENC_BLOCKS, NBLEN, total_cols)
    flat_ids = block_ids.reshape(SPANS * NEIGH).astype(jnp.int32)
    key_heads = jnp.take(key_blocks, flat_ids, axis=0).reshape(SPANS, NEIGH * NBLEN, HEADS, HD).astype(jnp.float32)
    value_heads = jnp.take(value_blocks, flat_ids, axis=0).reshape(SPANS, NEIGH * NBLEN, HEADS, HD).astype(jnp.float32)
    query_heads = query_rows.reshape(SPANS, CL, HEADS, HD).astype(jnp.float32)
    scores = jnp.einsum('cqhd,ckhd->chqk', query_heads, key_heads) * score_scale
    soft_weights = jax.nn.softmax(scores, axis=-1)
    soft_half = rounded(soft_weights)
    attended = jnp.einsum('chqk,ckhd->cqhd', soft_half, value_heads).astype(jnp.bfloat16).reshape(TOKENS, total_cols)
    layer_out = (x_rows.astype(jnp.float32) + group_sum(attended, out_proj)).astype(jnp.bfloat16)
    scaled = (token_scale[:, None] * cot_rows.astype(jnp.float32)).astype(jnp.bfloat16)
    attended_grad = jnp.dot(scaled, out_proj.T, preferred_element_type=jnp.float32).astype(jnp.bfloat16)
    grad_heads = attended_grad.reshape(SPANS, CL, HEADS, HD).astype(jnp.float32)
    soft_grad = jnp.einsum('cqhd,ckhd->chqk', grad_heads, value_heads)
    row_term = lax.optimization_barrier(jnp.sum(soft_grad * soft_weights, axis=-1, keepdims=True))
    score_grad = rounded(soft_weights * (soft_grad - row_term) * score_scale)
    query_grad = jnp.einsum('chqk,ckhd->cqhd', score_grad, key_heads).astype(jnp.bfloat16).reshape(TOKENS, total_cols)
    key_grad = jnp.einsum('chqk,cqhd->ckhd', score_grad, query_heads).astype(jnp.bfloat16)
    key_grad = key_grad.reshape(SPANS * NEIGH * NBLEN, total_cols)
    value_grad = jnp.einsum('chqk,cqhd->ckhd', soft_half, grad_heads).astype(jnp.bfloat16)
    value_grad = value_grad.reshape(SPANS * NEIGH * NBLEN, total_cols)
    input_grad = (scaled.astype(jnp.float32) + group_sum(query_grad, query_proj.T)).astype(jnp.bfloat16)
    grad_query = block_sum(x_rows, query_grad, TOK_DEV)
    grad_out = block_sum(attended, scaled, TOK_DEV)
    used_rows = jnp.take(enc_blocks, flat_ids, axis=0).reshape(SPANS * NEIGH * NBLEN, DE)
    grad_key = block_sum(used_rows, key_grad, CH_DEV * NEIGH * NBLEN)
    grad_value = block_sum(used_rows, value_grad, CH_DEV * NEIGH * NBLEN)
    group_width = HEAD_GROUP * HD
    use_grad = jnp.zeros((SPANS * NEIGH * NBLEN, DE), jnp.float32)
    for group_index in range(N_MP):
        column_start = group_index * group_width
        columns_end = column_start + group_width
        piece = jnp.dot(key_grad[:, column_start:columns_end], key_proj[:, column_start:columns_end].T, preferred_element_type=jnp.float32)
        piece = piece + jnp.dot(value_grad[:, column_start:columns_end], value_proj[:, column_start:columns_end].T, preferred_element_type=jnp.float32)
        use_grad = use_grad + rounded(piece)
    use_grad = use_grad.reshape(SPANS * NEIGH, NBLEN * DE)
    grad_enc = jax.ops.segment_sum(use_grad, flat_ids, num_segments=ENC_BLOCKS)
    grad_enc = grad_enc.reshape(ENC_BLOCKS, NBLEN, DE).astype(jnp.bfloat16)
    return (layer_out, input_grad, grad_query, grad_key, grad_value, grad_out, grad_enc)

def reference(x_in, cotangent, tok_weight, neighbours, w_query, w_key, w_value, w_out, encodings):
    results = []
    for section_index in range(SECTIONS):
        results.append(one_section(x_in[section_index], cotangent[section_index], tok_weight[section_index], neighbours[section_index], w_query[section_index], w_key[section_index], w_value[section_index], w_out[section_index], encodings[section_index]))
    stacked = [jnp.stack([entry[position] for entry in results]) for position in range(7)]
    next_input = jnp.roll(stacked[0], 1, axis=0)
    prev_grad = jnp.roll(stacked[1], -1, axis=0)
    return (next_input, prev_grad, stacked[2], stacked[3], stacked[4], stacked[5], stacked[6])
```

```python
import functools
import math

import jax
import jax.numpy as jnp
from jax import lax
from jax.experimental import pallas as pl
from jax.experimental.pallas import tpu as pltpu
from jax.sharding import PartitionSpec as P

HD = 128
NBLEN = 128
F32 = jnp.float32
BF16 = jnp.bfloat16


def shifted(value, axis, steps):
    count = lax.axis_size(axis)
    pairs = [(source, (source + steps) % count) for source in range(count)]
    return lax.ppermute(value, axis, pairs)


def along_z(value, steps):
    count = lax.axis_size("seq")
    pairs = [(source, (source + 2 * steps) % count) for source in range(count)]
    return lax.ppermute(value, "seq", pairs)


def other_core(value):
    count = lax.axis_size("seq")
    return lax.ppermute(value, "seq", [(source, source ^ 1) for source in range(count)])


def contract_rows(first_factor, second_factor):
    return lax.dot_general(
        first_factor, second_factor, (((0,), (0,)), ((), ())), preferred_element_type=F32
    )


def contract_cols(first_factor, second_factor):
    return lax.dot_general(
        first_factor, second_factor, (((1,), (1,)), ((), ())), preferred_element_type=F32
    )


def added(first, second):
    return (first.astype(F32) + second.astype(F32)).astype(BF16)


def gather_mp(part):
    half = part.shape[0] // 2
    behind = shifted(part, "mp", 1)
    ahead = shifted(part, "mp", -1)
    far_first = shifted(behind[:half], "mp", 1)
    far_second = shifted(ahead[half:], "mp", -1)
    return part, ahead, far_first, far_second, behind


def stacked(pieces):
    own, ahead, far_first, far_second, behind = pieces
    return jnp.stack([own, ahead, jnp.concatenate([far_first, far_second]), behind])


def exchanged_mp(pieces):
    first = shifted(pieces[1], "mp", 1)
    third = shifted(pieces[3], "mp", -1)
    second = shifted(pieces[2], "mp", 2)
    return pieces[0], first, second, third


def summed(terms):
    return sum(term.astype(F32) for term in terms)


def scatter_z(terms):
    half = terms.shape[1] // 2
    right = along_z(terms[4, :half], 1)
    left = along_z(terms[4, half:], -1)
    right = along_z(jnp.concatenate([added(terms[3, :half], right), terms[3, half:]]), 1)
    left = along_z(jnp.concatenate([terms[5, :half], added(terms[5, half:], left)]), -1)
    right = along_z(added(terms[2], right), 1)
    left = along_z(added(terms[6], left), -1)
    right = along_z(added(terms[1], right), 1)
    left = along_z(added(terms[7], left), -1)
    return summed([terms[0], right, left])


def whole(array):
    rank = len(array.shape)
    return pl.BlockSpec(array.shape, lambda *_: (0,) * rank)


def params(megabytes):
    return pltpu.CompilerParams(vmem_limit_bytes=megabytes * 2**20)


def cost(flops, moved):
    return pl.CostEstimate(flops=int(flops), bytes_accessed=int(moved), transcendentals=0)


def project_kernel(me, x, scaled, wq, wo, query, grad, query_sum, grad_sum):
    step = pl.program_id(0)

    @pl.when(step == 0)
    def _():
        query_sum[...] = jnp.zeros_like(query_sum)
        grad_sum[...] = jnp.zeros_like(grad_sum)

    query_sum[...] += jnp.dot(x[0], wq[...], preferred_element_type=F32)
    grad_sum[...] += contract_cols(scaled[0], wo[...])

    @pl.when(step == pl.num_programs(0) - 1)
    def _():
        query[...] = query_sum[...].astype(BF16)
        grad[...] = grad_sum[...].astype(BF16)


def project(me, x_stack, scaled_stack, wq, wo):
    parts, rows, width = x_stack.shape
    cols = wq.shape[1]
    ahead = lambda k, me: lax.rem(me[0] + k, parts)
    result = jax.ShapeDtypeStruct((rows, cols), BF16)
    return pl.pallas_call(
        project_kernel,
        out_shape=(result, result),
        grid_spec=pltpu.PrefetchScalarGridSpec(
            num_scalar_prefetch=1,
            grid=(parts,),
            in_specs=[
                pl.BlockSpec((1, rows, width), lambda k, me: (k, 0, 0)),
                pl.BlockSpec((1, rows, width), lambda k, me: (k, 0, 0)),
                pl.BlockSpec((width, cols), lambda k, me: (ahead(k, me), 0)),
                pl.BlockSpec((cols, width), lambda k, me: (0, ahead(k, me))),
            ],
            out_specs=[whole(result), whole(result)],
            scratch_shapes=[pltpu.VMEM((rows, cols), F32), pltpu.VMEM((rows, cols), F32)],
        ),
        compiler_params=params(24),
        cost_estimate=cost(4 * parts * rows * width * cols, 12 * 2**20),
        name="project",
    )(me, x_stack, scaled_stack, wq, wo)


def attend_kernel(scale, own, ahead, far_first, far_second, behind, wk, wv, query, grad,
                  attended, query_grad, key_grad, value_grad, used, t0, t1, t2, t3):
    span = pl.program_id(0)
    far = jnp.where(span < 2, far_first[...], far_second[...])
    part = own.shape[0]
    rows = jnp.concatenate([own[...], ahead[...], far, behind[...]], axis=0)
    used[...] = rows
    keys = jnp.dot(rows, wk[...], preferred_element_type=F32).astype(BF16)
    values = jnp.dot(rows, wv[...], preferred_element_type=F32).astype(BF16)
    query_all, grad_all = query[...], grad[...]
    heads = query_all.shape[1] // HD
    key_grads, value_grads = [], []
    for head in range(heads):
        cols = slice(head * HD, (head + 1) * HD)
        q, g, k, v = query_all[:, cols], grad_all[:, cols], keys[:, cols], values[:, cols]
        scores = contract_cols(q, k) * scale
        raised = jnp.exp(scores - jnp.max(scores, axis=-1, keepdims=True))
        weights = raised / jnp.sum(raised, axis=-1, keepdims=True)
        half = weights.astype(BF16)
        attended[:, cols] = jnp.dot(half, v, preferred_element_type=F32).astype(BF16)
        soft_grad = contract_cols(g, v)
        row_term = jnp.sum(soft_grad * weights, axis=-1, keepdims=True)
        score_grad = (weights * (soft_grad - row_term) * scale).astype(BF16)
        query_grad[:, cols] = jnp.dot(score_grad, k, preferred_element_type=F32).astype(BF16)
        key_grads.append(contract_rows(score_grad, q).astype(BF16))
        value_grads.append(contract_rows(half, g).astype(BF16))
    key_all = jnp.concatenate(key_grads, axis=1)
    value_all = jnp.concatenate(value_grads, axis=1)
    key_grad[...] = key_all
    value_grad[...] = value_all
    terms = contract_cols(key_all, wk[...]) + contract_cols(value_all, wv[...])
    for k, t in enumerate((t0, t1, t2, t3)):
        t[...] = terms[k * part : (k + 1) * part].astype(BF16)


def attend(pieces, wk, wv, query, grad, spans, scale):
    own, far_first = pieces[0], pieces[2]
    part, width = own.shape[0] // spans, own.shape[1]
    rows, cols = query.shape
    span_rows, span_keys = rows // spans, 4 * part
    by_span = lambda *shape: pl.BlockSpec(shape, lambda c: (c, 0))
    half = spans // 2
    out = lambda *shape: jax.ShapeDtypeStruct(shape, BF16)
    return pl.pallas_call(
        functools.partial(attend_kernel, scale),
        out_shape=(
            out(rows, cols), out(rows, cols),
            out(spans * span_keys, cols), out(spans * span_keys, cols),
            out(spans * span_keys, width),
            *[out(spans * part, width) for _ in range(4)],
        ),
        grid=(spans,),
        in_specs=[
            by_span(part, width), by_span(part, width),
            pl.BlockSpec((part, width), lambda c: (jnp.minimum(c, half - 1), 0)),
            pl.BlockSpec((part, width), lambda c: (jnp.maximum(c - half, 0), 0)),
            by_span(part, width),
            whole(wk), whole(wv),
            by_span(span_rows, cols), by_span(span_rows, cols),
        ],
        out_specs=(
            by_span(span_rows, cols), by_span(span_rows, cols),
            by_span(span_keys, cols), by_span(span_keys, cols),
            by_span(span_keys, width),
            *[by_span(part, width) for _ in range(4)],
        ),
        compiler_params=params(32),
        cost_estimate=cost(4.2e9, 12 * 2**20),
        name="attend",
    )(*pieces, wk, wv, query, grad)


def gradients_kernel(me, x, scaled, query_grad, attended, used, key_grad, value_grad, out,
                     query_t, attended_t, key_sum, value_sum):
    step = pl.program_id(0)

    @pl.when(step == 0)
    def _():
        query_t[...] = query_grad[...].T
        attended_t[...] = attended[...].T
        used_t = used[...].T
        key_sum[...] = jnp.dot(used_t, key_grad[...], preferred_element_type=F32)
        value_sum[...] = jnp.dot(used_t, value_grad[...], preferred_element_type=F32)

    group, width = query_t.shape[0], x.shape[2]
    out[0, :group] = jnp.dot(query_t[...], x[0], preferred_element_type=F32).astype(BF16)
    out[0, group : 2 * group] = jnp.dot(
        attended_t[...], scaled[0], preferred_element_type=F32
    ).astype(BF16)
    share = key_sum.shape[0] // pl.num_programs(0)
    slot = -(-share // 16) * 16
    owner = lax.rem(me[0] + step // 4, 4) * 4 + lax.rem(step, 4)
    here = pl.ds(pl.multiple_of(owner * share, 8), share)
    at = 2 * group
    for total in (key_sum, value_sum):
        rows = total[here, :]
        rows = jnp.concatenate([rows, jnp.zeros((slot - share, group), F32)]).astype(BF16)
        for col in range(0, group, width):
            out[0, at : at + slot] = rows[:, col : col + width]
            at += slot


def gradients(me, x_stack, scaled_stack, query_grad, attended, used, key_grad, value_grad, owners):
    parts, rows, width = x_stack.shape
    group = query_grad.shape[1]
    share = parts * width // owners
    per = owners // parts
    enc_width = used.shape[1]
    slot = -(-(enc_width // owners) // 16) * 16
    out_rows = 2 * group + 2 * slot * group // share
    return pl.pallas_call(
        gradients_kernel,
        out_shape=jax.ShapeDtypeStruct((owners, out_rows, share), BF16),
        grid_spec=pltpu.PrefetchScalarGridSpec(
            num_scalar_prefetch=1,
            grid=(owners,),
            in_specs=[
                pl.BlockSpec((1, rows, share), lambda s, me: (s // per, 0, lax.rem(s, per))),
                pl.BlockSpec((1, rows, share), lambda s, me: (s // per, 0, lax.rem(s, per))),
                whole(query_grad), whole(attended), whole(used), whole(key_grad), whole(value_grad),
            ],
            out_specs=pl.BlockSpec(
                (1, out_rows, share),
                lambda s, me: (lax.rem(me[0] + s // per, parts) * per + lax.rem(s, per), 0, 0),
            ),
            scratch_shapes=[
                pltpu.VMEM((group, rows), BF16), pltpu.VMEM((group, rows), BF16),
                pltpu.VMEM((enc_width, group), F32), pltpu.VMEM((enc_width, group), F32),
            ],
        ),
        compiler_params=params(40),
        cost_estimate=cost(4.0e9, 18 * 2**20),
        name="gradients",
    )(me, x_stack, scaled_stack, query_grad, attended, used, key_grad, value_grad)


def terms_kernel(me, attended, query_grad, wo, wq, *outs):
    step = pl.program_id(0)
    out = jnp.dot(attended[...], wo[...], preferred_element_type=F32).astype(BF16)
    back = contract_cols(query_grad[...], wq[...]).astype(BF16)
    for k in range(4):

        @pl.when(step == k)
        def _():
            outs[k][...] = out
            outs[4 + k][...] = back


def model_terms(me, attended, query_grad, wo, wq):
    rows, cols = attended.shape
    width = wo.shape[1] // 4
    ahead = lambda k, me: lax.rem(me[0] + k, 4)
    out = jax.ShapeDtypeStruct((rows, width), BF16)
    results = pl.pallas_call(
        terms_kernel,
        out_shape=[out] * 8,
        grid_spec=pltpu.PrefetchScalarGridSpec(
            num_scalar_prefetch=1,
            grid=(4,),
            in_specs=[
                whole(attended), whole(query_grad),
                pl.BlockSpec((cols, width), lambda k, me: (0, ahead(k, me))),
                pl.BlockSpec((width, cols), lambda k, me: (ahead(k, me), 0)),
            ],
            out_specs=[whole(out)] * 8,
        ),
        compiler_params=params(24),
        cost_estimate=cost(4 * 4 * rows * cols * width, 12 * 2**20),
        name="model_terms",
    )(me, attended, query_grad, wo, wq)
    return results[:4], results[4:]


def spread_kernel(where, first, second, third, fourth, kept, given):
    uses = first.shape[0]
    kept[...] = jnp.zeros_like(kept)
    given[...] = jnp.zeros_like(given)
    core, z = where[uses], where[uses + 1]
    chips, enc_dev = kept.shape[0], kept.shape[1]
    total = [summed([t[u] for t in (first, second, third, fourth)]) for u in range(uses)]
    for u in range(uses):
        block = where[u]
        value = total[u]
        for v in range(uses):
            if v != u:
                value = value + jnp.where(where[v] == block, total[v], 0.0)
        value = value.astype(BF16)
        owner = block // enc_dev
        slot = lax.rem(owner // 2 + chips - z, chips)

        @pl.when(lax.rem(owner, 2) == core)
        def _():
            kept[slot, lax.rem(block, enc_dev)] = value

        @pl.when(lax.rem(owner, 2) != core)
        def _():
            given[slot, lax.rem(block, enc_dev)] = value


def spread(where, terms, chips, enc_dev):
    uses, rows, width = terms[0].shape
    out = jax.ShapeDtypeStruct((chips, enc_dev, rows, width), BF16)
    return pl.pallas_call(
        spread_kernel,
        out_shape=(out, out),
        in_specs=[pl.BlockSpec(memory_space=pltpu.SMEM)] + [pl.BlockSpec(memory_space=pltpu.VMEM)] * 4,
        out_specs=(pl.BlockSpec(memory_space=pltpu.VMEM),) * 2,
        compiler_params=params(24),
        cost_estimate=cost(1e6, 6 * 2**20),
        name="spread",
    )(where, *terms)


def on_device(x_in, cotangent, tok_weight, neighbours, w_query, w_key, w_value, w_out, encodings):
    x_part = x_in[0]
    cot_part = cotangent[0]
    token_scale = tok_weight[0]
    query_proj = w_query[0]
    key_proj = w_key[0]
    value_proj = w_value[0]
    out_proj = w_out[0]
    enc_local = encodings[0]
    group_cols = query_proj.shape[1]
    enc_dev, enc_rows, enc_width = enc_local.shape
    span_count = neighbours.shape[1]
    use_count = span_count * neighbours.shape[2]
    owners = lax.axis_size("seq")
    chips = owners // 2
    me = lax.axis_index("mp").reshape(1)
    me_seq = lax.axis_index("seq")
    block_ids = neighbours[0].reshape(use_count)

    enc_all = lax.all_gather(enc_local, "seq", axis=0, tiled=True)
    scaled_part = (token_scale[:, None] * cot_part.astype(F32)).astype(BF16)
    x_stack = stacked(gather_mp(x_part))
    scaled_stack = stacked(gather_mp(scaled_part))
    query_rows, attended_grad = project(me, x_stack, scaled_stack, query_proj, out_proj)

    own_rows = jnp.take(enc_all, block_ids, axis=0).reshape(use_count * enc_rows, enc_width)
    attended, query_grad, key_grad, value_grad, used, *use_terms = attend(
        gather_mp(own_rows), key_proj, value_proj, query_rows, attended_grad,
        span_count, 1.0 / math.sqrt(HD),
    )
    use_terms = exchanged_mp([t.reshape(use_count, enc_rows, enc_width) for t in use_terms])

    grads = gradients(
        me, x_stack, scaled_stack, query_grad, attended, used, key_grad, value_grad, owners
    )
    grads, attended, query_grad = lax.optimization_barrier((grads, attended, query_grad))
    out_terms, input_terms = model_terms(me, attended, query_grad, out_proj, query_proj)
    grads = lax.psum_scatter(grads, "seq", scatter_dimension=0, tiled=True)[0]

    where = jnp.concatenate([block_ids, jnp.stack([me_seq % 2, me_seq // 2])])
    kept, given = spread(where, use_terms, chips, enc_dev)
    here = added(kept, other_core(given))
    grad_enc = scatter_z(here.reshape(chips, enc_dev * enc_rows, enc_width)).astype(BF16)
    grad_enc = grad_enc.reshape(enc_dev, enc_rows, enc_width)

    layer_out = (x_part.astype(F32) + summed(exchanged_mp(out_terms))).astype(BF16)
    next_input = shifted(layer_out, "section", 1)
    input_grad = (scaled_part.astype(F32) + summed(exchanged_mp(input_terms))).astype(BF16)
    prev_grad = shifted(input_grad, "section", -1)

    enc_share = enc_width // owners
    slot = -(-enc_share // 16) * 16
    grad_query = grads[:group_cols].T
    grad_out = grads[group_cols : 2 * group_cols]
    key_value = grads[2 * group_cols :].reshape(2, -1, slot, grads.shape[1])[:, :, :enc_share]
    key_value = key_value.transpose(0, 2, 1, 3).reshape(2, enc_share, group_cols)
    return (
        next_input[None],
        prev_grad[None],
        grad_query[None],
        key_value[:1],
        key_value[1:],
        grad_out[None],
        grad_enc[None],
    )


def solution(mesh):
    placed = (
        P("section", "seq", "mp"),
        P("section", "seq", "mp"),
        P("section", "seq"),
        P("section", "seq", None),
        P("section", None, "mp"),
        P("section", None, "mp"),
        P("section", None, "mp"),
        P("section", "mp", None),
        P("section", "seq", "mp", None),
    )
    return jax.shard_map(
        on_device,
        mesh=mesh,
        in_specs=placed,
        out_specs=(
            P("section", "seq", "mp"),
            P("section", "seq", "mp"),
            P("section", "seq", "mp"),
            P("section", "seq", "mp"),
            P("section", "seq", "mp"),
            P("section", "mp", "seq"),
            P("section", "seq", "mp", None),
        ),
        check_vma=False,
    )
```

```python
import functools
import math

import jax
import jax.numpy as jnp
from jax import lax
from jax.experimental import pallas as pl
from jax.experimental.pallas import tpu as pltpu
from jax.sharding import PartitionSpec as P

HD = 128
NBLEN = 128
F32 = jnp.float32
BF16 = jnp.bfloat16


def shifted(value, axis, steps):
    count = lax.axis_size(axis)
    pairs = [(source, (source + steps) % count) for source in range(count)]
    return lax.ppermute(value, axis, pairs)


def along_z(value, steps):
    count = lax.axis_size("seq")
    pairs = [(source, (source + 2 * steps) % count) for source in range(count)]
    return lax.ppermute(value, "seq", pairs)


def other_core(value):
    count = lax.axis_size("seq")
    return lax.ppermute(value, "seq", [(source, source ^ 1) for source in range(count)])


def contract_rows(first_factor, second_factor):
    return lax.dot_general(
        first_factor, second_factor, (((0,), (0,)), ((), ())), preferred_element_type=F32
    )


def contract_cols(first_factor, second_factor):
    return lax.dot_general(
        first_factor, second_factor, (((1,), (1,)), ((), ())), preferred_element_type=F32
    )


def added(first, second):
    return (first.astype(F32) + second.astype(F32)).astype(BF16)


def gather_mp(part, beside=None):
    half = part.shape[0] // 2
    behind = shifted(part, "mp", 1)
    ahead = shifted(part, "mp", -1)
    if beside is not None:
        behind, ahead, beside = lax.optimization_barrier((behind, ahead, beside))
    far_first = shifted(behind[:half], "mp", 1)
    far_second = shifted(ahead[half:], "mp", -1)
    pieces = part, ahead, far_first, far_second, behind
    return pieces if beside is None else (pieces, beside)


def pick_kernel(block_ids, blocks, out, done):
    copies = [
        pltpu.make_async_copy(blocks.at[block_ids[u]], out.at[u], done.at[u])
        for u in range(out.shape[0])
    ]
    for copy in copies:
        copy.start()
    for copy in copies:
        copy.wait()


def pick(block_ids, blocks):
    uses = block_ids.shape[0]
    return pl.pallas_call(
        pick_kernel,
        out_shape=jax.ShapeDtypeStruct((uses, *blocks.shape[1:]), BF16),
        in_specs=[pl.BlockSpec(memory_space=pltpu.SMEM), pl.BlockSpec(memory_space=pltpu.HBM)],
        out_specs=pl.BlockSpec(memory_space=pltpu.VMEM),
        scratch_shapes=[pltpu.SemaphoreType.DMA((uses,))],
        compiler_params=params(4),
        cost_estimate=cost(1e6, 2**20),
        name="pick",
    )(block_ids, blocks)


def stacked(pieces):
    own, ahead, far_first, far_second, behind = pieces
    return jnp.stack([own, ahead, jnp.concatenate([far_first, far_second]), behind])


def exchanged_mp(pieces):
    first = shifted(pieces[1], "mp", 1)
    third = shifted(pieces[3], "mp", -1)
    second = shifted(pieces[2], "mp", 2)
    return pieces[0], first, second, third


def summed(terms):
    return sum(term.astype(F32) for term in terms)


def scatter_z_first(terms):
    half = terms.shape[1] // 2
    return along_z(terms[4, :half], 1), along_z(terms[4, half:], -1)


def scatter_z_middle(terms, arrived):
    right, left = arrived
    half = terms.shape[1] // 2
    right = along_z(jnp.concatenate([added(terms[3, :half], right), terms[3, half:]]), 1)
    left = along_z(jnp.concatenate([terms[5, :half], added(terms[5, half:], left)]), -1)
    return along_z(added(terms[2], right), 1), along_z(added(terms[6], left), -1)


def scatter_z_last(terms, arrived):
    right, left = arrived
    return along_z(added(terms[1], right), 1), along_z(added(terms[7], left), -1)


def unpack_kernel(packed, query, key, value, out):
    group, share = query.shape[1], query.shape[0]
    query[...] = packed[:group].T
    out[...] = packed[group : 2 * group]
    rows = key.shape[0]
    slot = -(-rows // 16) * 16
    at = 2 * group
    for result in (key, value):
        for col in range(0, group, share):
            result[:, col : col + share] = packed[at : at + slot][:rows]
            at += slot


def unpacked(packed, group, enc_share):
    share = packed.shape[1]
    out = lambda *shape: jax.ShapeDtypeStruct(shape, BF16)
    in_vmem = pl.BlockSpec(memory_space=pltpu.VMEM)
    return pl.pallas_call(
        unpack_kernel,
        out_shape=(out(share, group), out(enc_share, group), out(enc_share, group), out(group, share)),
        in_specs=[in_vmem],
        out_specs=(in_vmem,) * 4,
        compiler_params=params(8),
        cost_estimate=cost(1e6, 2 * 2**20),
        name="unpack",
    )(packed)


def whole(array):
    rank = len(array.shape)
    return pl.BlockSpec(array.shape, lambda *_: (0,) * rank)


def params(megabytes):
    return pltpu.CompilerParams(vmem_limit_bytes=megabytes * 2**20)


def cost(flops, moved):
    return pl.CostEstimate(flops=int(flops), bytes_accessed=int(moved), transcendentals=0)


def project_kernel(me, x, scaled, wq, wo, query, grad, query_sum, grad_sum):
    step = pl.program_id(0)

    @pl.when(step == 0)
    def _():
        query_sum[...] = jnp.zeros_like(query_sum)
        grad_sum[...] = jnp.zeros_like(grad_sum)

    query_sum[...] += jnp.dot(x[0], wq[...], preferred_element_type=F32)
    grad_sum[...] += contract_cols(scaled[0], wo[...])

    @pl.when(step == pl.num_programs(0) - 1)
    def _():
        query[...] = query_sum[...].astype(BF16)
        grad[...] = grad_sum[...].astype(BF16)


def project(me, x_stack, scaled_stack, wq, wo):
    parts, rows, width = x_stack.shape
    cols = wq.shape[1]
    ahead = lambda k, me: lax.rem(me[0] + k, parts)
    result = jax.ShapeDtypeStruct((rows, cols), BF16)
    return pl.pallas_call(
        project_kernel,
        out_shape=(result, result),
        grid_spec=pltpu.PrefetchScalarGridSpec(
            num_scalar_prefetch=1,
            grid=(parts,),
            in_specs=[
                pl.BlockSpec((1, rows, width), lambda k, me: (k, 0, 0)),
                pl.BlockSpec((1, rows, width), lambda k, me: (k, 0, 0)),
                pl.BlockSpec((width, cols), lambda k, me: (ahead(k, me), 0)),
                pl.BlockSpec((cols, width), lambda k, me: (0, ahead(k, me))),
            ],
            out_specs=[whole(result), whole(result)],
            scratch_shapes=[pltpu.VMEM((rows, cols), F32), pltpu.VMEM((rows, cols), F32)],
        ),
        compiler_params=params(16),
        cost_estimate=cost(1e6, 2**16),
        name="project",
    )(me, x_stack, scaled_stack, wq, wo)


def attend_kernel(scale, span_rows, own, ahead, far_first, far_second, behind, wk, wv, query, grad,
                  attended, query_grad, key_grad, value_grad, used, t0, t1, t2, t3):
    far = jnp.where(pl.program_id(0) == 0, far_first[...], far_second[...])
    spans = query.shape[0] // span_rows
    part = far.shape[0] // spans
    span_keys = 4 * part
    pieces = (own[...], ahead[...], far, behind[...])
    rows = jnp.concatenate(
        [piece[c * part : (c + 1) * part] for c in range(spans) for piece in pieces], axis=0
    )
    used[...] = rows
    keys = jnp.dot(rows, wk[...], preferred_element_type=F32).astype(BF16)
    values = jnp.dot(rows, wv[...], preferred_element_type=F32).astype(BF16)
    query_all, grad_all = query[...], grad[...]
    for c in range(spans):
        at, key_at = slice(c * span_rows, (c + 1) * span_rows), slice(c * span_keys, (c + 1) * span_keys)
        for head in range(query_all.shape[1] // HD):
            cols = slice(head * HD, (head + 1) * HD)
            q, g = query_all[at, cols], grad_all[at, cols]
            k, v = keys[key_at, cols], values[key_at, cols]
            scores = contract_cols(q, k) * scale
            raised = jnp.exp(scores - jnp.max(scores, axis=-1, keepdims=True))
            weights = raised / jnp.sum(raised, axis=-1, keepdims=True)
            half = weights.astype(BF16)
            attended[at, cols] = jnp.dot(half, v, preferred_element_type=F32).astype(BF16)
            soft_grad = contract_cols(g, v)
            row_term = jnp.sum(soft_grad * weights, axis=-1, keepdims=True)
            score_grad = (weights * (soft_grad - row_term) * scale).astype(BF16)
            query_grad[at, cols] = jnp.dot(score_grad, k, preferred_element_type=F32).astype(BF16)
            key_grad[key_at, cols] = contract_rows(score_grad, q).astype(BF16)
            value_grad[key_at, cols] = contract_rows(half, g).astype(BF16)
    terms = contract_cols(key_grad[...], wk[...]) + contract_cols(value_grad[...], wv[...])
    terms = terms.astype(BF16)
    for c in range(spans):
        for k, t in enumerate((t0, t1, t2, t3)):
            start = c * span_keys + k * part
            t[c * part : (c + 1) * part] = terms[start : start + part]


def attend(pieces, wk, wv, query, grad, spans, scale):
    own, far_first = pieces[0], pieces[2]
    steps = 2
    part, width = own.shape[0] // steps, own.shape[1]
    rows, cols = query.shape
    by_step = lambda height, breadth: pl.BlockSpec((height, breadth), lambda c: (c, 0))
    out = lambda *shape: jax.ShapeDtypeStruct(shape, BF16)
    return pl.pallas_call(
        functools.partial(attend_kernel, scale, rows // spans),
        out_shape=(
            out(rows, cols), out(rows, cols),
            out(4 * steps * part, cols), out(4 * steps * part, cols),
            out(4 * steps * part, width),
            *[out(steps * part, width) for _ in range(4)],
        ),
        grid=(steps,),
        in_specs=[
            by_step(part, width), by_step(part, width), whole(far_first), whole(far_first),
            by_step(part, width),
            whole(wk), whole(wv),
            by_step(rows // steps, cols), by_step(rows // steps, cols),
        ],
        out_specs=(
            by_step(rows // steps, cols), by_step(rows // steps, cols),
            by_step(4 * part, cols), by_step(4 * part, cols),
            by_step(4 * part, width),
            *[by_step(part, width) for _ in range(4)],
        ),
        compiler_params=params(28),
        cost_estimate=cost(4.2e9, 12 * 2**20),
        name="attend",
    )(*pieces, wk, wv, query, grad)


def gradients_kernel(me, x, scaled, query_grad, attended, used, key_grad, value_grad, out,
                     query_t, attended_t, key_sum, value_sum):
    step, parts = pl.program_id(0), pl.num_programs(0)

    @pl.when(step == 0)
    def _():
        query_t[...] = query_grad[...].T
        attended_t[...] = attended[...].T
        used_t = used[...].T
        key_sum[...] = jnp.dot(used_t, key_grad[...], preferred_element_type=F32)
        value_sum[...] = jnp.dot(used_t, value_grad[...], preferred_element_type=F32)

    group, (per, _, width) = query_t.shape[0], out.shape
    share = key_sum.shape[0] // (parts * per)
    slot = -(-share // 16) * 16
    first = lax.rem(me[0] + step, parts) * per
    for i in range(per):
        cols = slice(i * width, (i + 1) * width)
        out[i, :group] = jnp.dot(
            query_t[...], x[0, :, cols], preferred_element_type=F32
        ).astype(BF16)
        out[i, group : 2 * group] = jnp.dot(
            attended_t[...], scaled[0, :, cols], preferred_element_type=F32
        ).astype(BF16)
        here = pl.ds(pl.multiple_of((first + i) * share, 8), share)
        at = 2 * group
        for total in (key_sum, value_sum):
            rows = total[here, :]
            rows = jnp.concatenate([rows, jnp.zeros((slot - share, group), F32)]).astype(BF16)
            for col in range(0, group, width):
                out[i, at : at + slot] = rows[:, col : col + width]
                at += slot


def gradients(me, x_stack, scaled_stack, query_grad, attended, used, key_grad, value_grad, owners):
    parts, rows, width = x_stack.shape
    group = query_grad.shape[1]
    share = parts * width // owners
    per = owners // parts
    enc_width = used.shape[1]
    slot = -(-(enc_width // owners) // 16) * 16
    out_rows = 2 * group + 2 * slot * group // share
    by_step = pl.BlockSpec((1, rows, width), lambda s, me: (s, 0, 0))
    return pl.pallas_call(
        gradients_kernel,
        out_shape=jax.ShapeDtypeStruct((owners, out_rows, share), BF16),
        grid_spec=pltpu.PrefetchScalarGridSpec(
            num_scalar_prefetch=1,
            grid=(parts,),
            in_specs=[
                by_step, by_step,
                whole(query_grad), whole(attended), whole(used), whole(key_grad), whole(value_grad),
            ],
            out_specs=pl.BlockSpec(
                (per, out_rows, share), lambda s, me: (lax.rem(me[0] + s, parts), 0, 0)
            ),
            scratch_shapes=[
                pltpu.VMEM((group, rows), BF16), pltpu.VMEM((group, rows), BF16),
                pltpu.VMEM((enc_width, group), F32), pltpu.VMEM((enc_width, group), F32),
            ],
        ),
        compiler_params=params(44),
        cost_estimate=cost(8e9, 36 * 2**20),
        name="gradients",
    )(me, x_stack, scaled_stack, query_grad, attended, used, key_grad, value_grad)


def terms_kernel(me, attended, query_grad, wo, wq, *outs):
    step = pl.program_id(0)
    out = jnp.dot(attended[...], wo[...], preferred_element_type=F32).astype(BF16)
    back = contract_cols(query_grad[...], wq[...]).astype(BF16)
    for k in range(4):

        @pl.when(step == k)
        def _():
            outs[k][0] = out
            outs[k][1] = back


def model_terms(me, attended, query_grad, wo, wq):
    rows, cols = attended.shape
    width = wo.shape[1] // 4
    ahead = lambda k, me: lax.rem(me[0] + k, 4)
    out = jax.ShapeDtypeStruct((2, rows, width), BF16)
    return pl.pallas_call(
        terms_kernel,
        out_shape=[out] * 4,
        grid_spec=pltpu.PrefetchScalarGridSpec(
            num_scalar_prefetch=1,
            grid=(4,),
            in_specs=[
                whole(attended), whole(query_grad),
                pl.BlockSpec((cols, width), lambda k, me: (0, ahead(k, me))),
                pl.BlockSpec((width, cols), lambda k, me: (ahead(k, me), 0)),
            ],
            out_specs=[whole(out)] * 4,
        ),
        compiler_params=params(24),
        cost_estimate=cost(1e6, 2**16),
        name="model_terms",
    )(me, attended, query_grad, wo, wq)


def spread_kernel(where, first, second, third, fourth, kept, given):
    uses = first.shape[0]
    kept[...] = jnp.zeros_like(kept)
    given[...] = jnp.zeros_like(given)
    core, z = where[uses], where[uses + 1]
    chips, enc_dev = kept.shape[0], kept.shape[1]
    total = [summed([t[u] for t in (first, second, third, fourth)]) for u in range(uses)]
    for u in range(uses):
        block = where[u]
        value = total[u]
        for v in range(uses):
            if v != u:
                value = value + jnp.where(where[v] == block, total[v], 0.0)
        value = value.astype(BF16)
        owner = block // enc_dev
        slot = lax.rem(owner // 2 + chips - z, chips)

        @pl.when(lax.rem(owner, 2) == core)
        def _():
            kept[slot, lax.rem(block, enc_dev)] = value

        @pl.when(lax.rem(owner, 2) != core)
        def _():
            given[slot, lax.rem(block, enc_dev)] = value


def spread(where, terms, chips, enc_dev):
    uses, rows, width = terms[0].shape
    out = jax.ShapeDtypeStruct((chips, enc_dev, rows, width), BF16)
    return pl.pallas_call(
        spread_kernel,
        out_shape=(out, out),
        in_specs=[pl.BlockSpec(memory_space=pltpu.SMEM)] + [pl.BlockSpec(memory_space=pltpu.VMEM)] * 4,
        out_specs=(pl.BlockSpec(memory_space=pltpu.VMEM),) * 2,
        compiler_params=params(24),
        cost_estimate=cost(1e11, 2**20),
        name="spread",
    )(where, *terms)


def on_device(x_in, cotangent, tok_weight, neighbours, w_query, w_key, w_value, w_out, encodings):
    x_part = x_in[0]
    cot_part = cotangent[0]
    token_scale = tok_weight[0]
    query_proj = w_query[0]
    key_proj = w_key[0]
    value_proj = w_value[0]
    out_proj = w_out[0]
    enc_local = encodings[0]
    group_cols = query_proj.shape[1]
    enc_dev, enc_rows, enc_width = enc_local.shape
    span_count = neighbours.shape[1]
    use_count = span_count * neighbours.shape[2]
    owners = lax.axis_size("seq")
    chips = owners // 2
    me = lax.axis_index("mp").reshape(1)
    me_seq = lax.axis_index("seq")
    block_ids = neighbours[0].reshape(use_count)

    where = jnp.concatenate([block_ids, jnp.stack([me_seq % 2, me_seq // 2])])
    scaled_part = (token_scale[:, None] * cot_part.astype(F32)).astype(BF16)
    enc_all = lax.all_gather(enc_local, "seq", axis=0, tiled=True)
    x_stack = stacked(gather_mp(x_part))
    scaled_stack = stacked(gather_mp(scaled_part))
    query_rows, attended_grad = project(me, x_stack, scaled_stack, query_proj, out_proj)

    own_rows = pick(block_ids, enc_all).reshape(use_count * enc_rows, enc_width)
    used_pieces, (query_rows, attended_grad) = gather_mp(own_rows, (query_rows, attended_grad))
    attended, query_grad, key_grad, value_grad, used, *use_terms = attend(
        used_pieces, key_proj, value_proj, query_rows, attended_grad,
        span_count, 1.0 / math.sqrt(HD),
    )
    use_terms = [t.reshape(use_count, enc_rows, enc_width) for t in use_terms]
    grads = gradients(
        me, x_stack, scaled_stack, query_grad, attended, used, key_grad, value_grad, owners
    )
    use_terms = exchanged_mp(use_terms)
    grads, attended, query_grad = lax.optimization_barrier((grads, attended, query_grad))
    terms = model_terms(me, attended, query_grad, out_proj, query_proj)
    grads = lax.psum_scatter(grads, "seq", scatter_dimension=0, tiled=True)[0]

    use_terms, terms = lax.optimization_barrier((use_terms, tuple(terms)))
    kept, given = spread(where, use_terms, chips, enc_dev)
    first, third = shifted(terms[1], "mp", 1), shifted(terms[3], "mp", -1)
    here = added(kept, other_core(given)).reshape(chips, enc_dev * enc_rows, enc_width)
    arrived, first, third, across = lax.optimization_barrier(
        (scatter_z_first(here), first, third, terms[2])
    )
    second = shifted(across, "mp", 2)
    arrived, second = lax.optimization_barrier((scatter_z_middle(here, arrived), second))
    terms = (terms[0], first, second, third)
    next_input = shifted(summed([x_part, *[t[0] for t in terms]]).astype(BF16), "section", 1)
    prev_grad = shifted(summed([scaled_part, *[t[1] for t in terms]]).astype(BF16), "section", -1)
    arrived = scatter_z_last(here, arrived)
    grad_enc = summed([here[0], *arrived]).astype(BF16)
    grad_enc = grad_enc.reshape(enc_dev, enc_rows, enc_width)

    grad_query, grad_key, grad_value, grad_out = unpacked(grads, group_cols, enc_width // owners)
    return (
        next_input[None],
        prev_grad[None],
        grad_query[None],
        grad_key[None],
        grad_value[None],
        grad_out[None],
        grad_enc[None],
    )


def solution(mesh):
    placed = (
        P("section", "seq", "mp"),
        P("section", "seq", "mp"),
        P("section", "seq"),
        P("section", "seq", None),
        P("section", None, "mp"),
        P("section", None, "mp"),
        P("section", None, "mp"),
        P("section", "mp", None),
        P("section", "seq", "mp", None),
    )
    return jax.shard_map(
        on_device,
        mesh=mesh,
        in_specs=placed,
        out_specs=(
            P("section", "seq", "mp"),
            P("section", "seq", "mp"),
            P("section", "seq", "mp"),
            P("section", "seq", "mp"),
            P("section", "seq", "mp"),
            P("section", "mp", "seq"),
            P("section", "seq", "mp", None),
        ),
        check_vma=False,
    )
```

```python
import functools
import math

import jax
import jax.numpy as jnp
from jax import lax
from jax.experimental import pallas as pl
from jax.experimental.pallas import tpu as pltpu
from jax.sharding import PartitionSpec as P

HD = 128
NBLEN = 128
F32 = jnp.float32
BF16 = jnp.bfloat16


def shifted(value, axis, steps):
    count = lax.axis_size(axis)
    pairs = [(source, (source + steps) % count) for source in range(count)]
    return lax.ppermute(value, axis, pairs)


def along_z(value, steps):
    count = lax.axis_size("seq")
    pairs = [(source, (source + 2 * steps) % count) for source in range(count)]
    return lax.ppermute(value, "seq", pairs)


def other_core(value):
    count = lax.axis_size("seq")
    return lax.ppermute(value, "seq", [(source, source ^ 1) for source in range(count)])


def contract_rows(first_factor, second_factor):
    return lax.dot_general(
        first_factor, second_factor, (((0,), (0,)), ((), ())), preferred_element_type=F32
    )


def contract_cols(first_factor, second_factor):
    return lax.dot_general(
        first_factor, second_factor, (((1,), (1,)), ((), ())), preferred_element_type=F32
    )


def added(first, second):
    return (first.astype(F32) + second.astype(F32)).astype(BF16)


def gather_mp(part):
    half = part.shape[0] // 2
    behind = shifted(part, "mp", 1)
    ahead = shifted(part, "mp", -1)
    far_first = shifted(behind[:half], "mp", 1)
    far_second = shifted(ahead[half:], "mp", -1)
    return part, ahead, far_first, far_second, behind


def pick_kernel(block_ids, blocks, out, done):
    copies = [
        pltpu.make_async_copy(blocks.at[block_ids[u]], out.at[u], done.at[u])
        for u in range(out.shape[0])
    ]
    for copy in copies:
        copy.start()
    for copy in copies:
        copy.wait()


def pick(block_ids, blocks):
    uses = block_ids.shape[0]
    return pl.pallas_call(
        pick_kernel,
        out_shape=jax.ShapeDtypeStruct((uses, *blocks.shape[1:]), BF16),
        in_specs=[pl.BlockSpec(memory_space=pltpu.SMEM), pl.BlockSpec(memory_space=pltpu.HBM)],
        out_specs=pl.BlockSpec(memory_space=pltpu.VMEM),
        scratch_shapes=[pltpu.SemaphoreType.DMA((uses,))],
        compiler_params=params(4),
        cost_estimate=cost(1e6, 2**20),
        name="pick",
    )(block_ids, in_hbm(blocks))


def stacked(pieces):
    own, ahead, far_first, far_second, behind = pieces
    return jnp.stack([own, ahead, jnp.concatenate([far_first, far_second]), behind])


def exchanged_mp(pieces):
    first = shifted(pieces[1], "mp", 1)
    third = shifted(pieces[3], "mp", -1)
    second = shifted(pieces[2], "mp", 2)
    return pieces[0], first, second, third


def summed(terms):
    return sum(term.astype(F32) for term in terms)


def scatter_z_first(terms):
    half = terms.shape[1] // 2
    return along_z(terms[4, :half], 1), along_z(terms[4, half:], -1)


def scatter_z_middle(terms, arrived):
    right, left = arrived
    half = terms.shape[1] // 2
    right = along_z(jnp.concatenate([added(terms[3, :half], right), terms[3, half:]]), 1)
    left = along_z(jnp.concatenate([terms[5, :half], added(terms[5, half:], left)]), -1)
    return along_z(added(terms[2], right), 1), along_z(added(terms[6], left), -1)


def scatter_z_last(terms, arrived):
    right, left = arrived
    return along_z(added(terms[1], right), 1), along_z(added(terms[7], left), -1)


def unpack_kernel(packed, query, key, value, out):
    group, share = query.shape[1], query.shape[0]
    query[...] = packed[:group].T
    out[...] = packed[group : 2 * group]
    rows = key.shape[0]
    at = 2 * group
    for col in range(0, group, share):
        pair = packed[at : at + 2 * rows].astype(F32)
        key[:, col : col + share] = pair[:rows].astype(BF16)
        value[:, col : col + share] = pair[rows:].astype(BF16)
        at += 2 * rows


def unpacked(packed, group, enc_share):
    share = packed.shape[1]
    out = lambda *shape: jax.ShapeDtypeStruct(shape, BF16)
    in_vmem = pl.BlockSpec(memory_space=pltpu.VMEM)
    return pl.pallas_call(
        unpack_kernel,
        out_shape=(out(share, group), out(enc_share, group), out(enc_share, group), out(group, share)),
        in_specs=[in_vmem],
        out_specs=(in_vmem,) * 4,
        compiler_params=params(8),
        cost_estimate=cost(1e6, 2 * 2**20),
        name="unpack",
    )(packed)


def whole(array):
    rank = len(array.shape)
    return pl.BlockSpec(array.shape, lambda *_: (0,) * rank)


def in_hbm(array):
    return pltpu.with_memory_space_constraint(array, pltpu.HBM)


def params(megabytes):
    return pltpu.CompilerParams(vmem_limit_bytes=megabytes * 2**20)


def cost(flops, moved):
    return pl.CostEstimate(flops=int(flops), bytes_accessed=int(moved), transcendentals=0)


def project_kernel(me, x, scaled, wq, wo, query, grad, query_sum, grad_sum):
    step = pl.program_id(0)

    @pl.when(step == 0)
    def _():
        query_sum[...] = jnp.zeros_like(query_sum)
        grad_sum[...] = jnp.zeros_like(grad_sum)

    query_sum[...] += jnp.dot(x[0], wq[...], preferred_element_type=F32)
    grad_sum[...] += contract_cols(scaled[0], wo[...])

    @pl.when(step == pl.num_programs(0) - 1)
    def _():
        query[...] = query_sum[...].astype(BF16)
        grad[...] = grad_sum[...].astype(BF16)


def project(me, x_stack, scaled_stack, wq, wo):
    parts, rows, width = x_stack.shape
    cols = wq.shape[1]
    ahead = lambda k, me: lax.rem(me[0] + k, parts)
    result = jax.ShapeDtypeStruct((rows, cols), BF16)
    return pl.pallas_call(
        project_kernel,
        out_shape=(result, result),
        grid_spec=pltpu.PrefetchScalarGridSpec(
            num_scalar_prefetch=1,
            grid=(parts,),
            in_specs=[
                pl.BlockSpec((1, rows, width), lambda k, me: (k, 0, 0)),
                pl.BlockSpec((1, rows, width), lambda k, me: (k, 0, 0)),
                pl.BlockSpec((width, cols), lambda k, me: (ahead(k, me), 0)),
                pl.BlockSpec((cols, width), lambda k, me: (0, ahead(k, me))),
            ],
            out_specs=[whole(result), whole(result)],
            scratch_shapes=[pltpu.VMEM((rows, cols), F32), pltpu.VMEM((rows, cols), F32)],
        ),
        compiler_params=params(16),
        cost_estimate=cost(1e6, 2**16),
        name="project",
    )(me, x_stack, scaled_stack, wq, wo)


def attend_kernel(scale, span_rows, own, ahead, far_first, far_second, behind, wk, wv, query, grad,
                  attended, query_grad, key_grad, value_grad, used):
    far = jnp.where(pl.program_id(0) == 0, far_first[...], far_second[...])
    spans = query.shape[0] // span_rows
    part = far.shape[0] // spans
    span_keys = 4 * part
    pieces = (own[...], ahead[...], far, behind[...])
    rows = jnp.concatenate(
        [piece[c * part : (c + 1) * part] for c in range(spans) for piece in pieces], axis=0
    )
    used[...] = rows
    keys = jnp.dot(rows, wk[...], preferred_element_type=F32).astype(BF16)
    values = jnp.dot(rows, wv[...], preferred_element_type=F32).astype(BF16)
    query_all, grad_all = query[...], grad[...]
    for c in range(spans):
        at, key_at = slice(c * span_rows, (c + 1) * span_rows), slice(c * span_keys, (c + 1) * span_keys)
        for head in range(query_all.shape[1] // HD):
            cols = slice(head * HD, (head + 1) * HD)
            q, g = query_all[at, cols], grad_all[at, cols]
            k, v = keys[key_at, cols], values[key_at, cols]
            scores = contract_cols(q, k) * scale
            raised = jnp.exp(scores - jnp.max(scores, axis=-1, keepdims=True))
            weights = raised / jnp.sum(raised, axis=-1, keepdims=True)
            half = weights.astype(BF16)
            attended[at, cols] = jnp.dot(half, v, preferred_element_type=F32).astype(BF16)
            soft_grad = contract_cols(g, v)
            row_term = jnp.sum(soft_grad * weights, axis=-1, keepdims=True)
            score_grad = (weights * (soft_grad - row_term) * scale).astype(BF16)
            query_grad[at, cols] = jnp.dot(score_grad, k, preferred_element_type=F32).astype(BF16)
            key_grad[key_at, cols] = contract_rows(score_grad, q).astype(BF16)
            value_grad[key_at, cols] = contract_rows(half, g).astype(BF16)


def use_terms_kernel(spans, key_grad, value_grad, wk, wv, *outs):
    terms = contract_cols(key_grad[...], wk[...]) + contract_cols(value_grad[...], wv[...])
    terms = terms.astype(BF16)
    part = outs[0].shape[0] // spans
    for c in range(spans):
        for k, out in enumerate(outs):
            start = (4 * c + k) * part
            out[c * part : (c + 1) * part] = terms[start : start + part]


def use_gradients(key_grad, value_grad, wk, wv, spans):
    steps = 2
    rows, cols = key_grad.shape
    width = wk.shape[0]
    by_step = lambda height, breadth: pl.BlockSpec((height, breadth), lambda c: (c, 0))
    return pl.pallas_call(
        functools.partial(use_terms_kernel, spans // steps),
        out_shape=[jax.ShapeDtypeStruct((rows // 4, width), BF16)] * 4,
        grid=(steps,),
        in_specs=[by_step(rows // steps, cols), by_step(rows // steps, cols), whole(wk), whole(wv)],
        out_specs=[by_step(rows // 4 // steps, width)] * 4,
        compiler_params=params(20),
        cost_estimate=cost(1e6, 2**16),
        name="use_gradients",
    )(key_grad, value_grad, wk, wv)


def attend(pieces, wk, wv, query, grad, spans, scale):
    own, far_first = pieces[0], pieces[2]
    steps = 2
    part, width = own.shape[0] // steps, own.shape[1]
    rows, cols = query.shape
    by_step = lambda height, breadth: pl.BlockSpec((height, breadth), lambda c: (c, 0))
    out = lambda *shape: jax.ShapeDtypeStruct(shape, BF16)
    return pl.pallas_call(
        functools.partial(attend_kernel, scale, rows // spans),
        out_shape=(
            out(rows, cols), out(rows, cols),
            out(4 * steps * part, cols), out(4 * steps * part, cols),
            out(4 * steps * part, width),
        ),
        grid=(steps,),
        in_specs=[
            by_step(part, width), by_step(part, width), whole(far_first), whole(far_first),
            by_step(part, width),
            whole(wk), whole(wv),
            by_step(rows // steps, cols), by_step(rows // steps, cols),
        ],
        out_specs=(
            by_step(rows // steps, cols), by_step(rows // steps, cols),
            by_step(4 * part, cols), by_step(4 * part, cols),
            by_step(4 * part, width),
        ),
        compiler_params=params(28),
        cost_estimate=cost(4.2e9, 12 * 2**20),
        name="attend",
    )(*pieces, wk, wv, query, grad)


def gradients_kernel(me, x, scaled, query_grad, attended, used, key_grad, value_grad, out,
                     query_t, attended_t, key_sum, value_sum):
    step, parts = pl.program_id(0), pl.num_programs(0)

    @pl.when(step == 0)
    def _():
        query_t[...] = query_grad[...].T
        attended_t[...] = attended[...].T
        used_t = used[...].T
        key_sum[...] = jnp.dot(used_t, key_grad[...], preferred_element_type=F32)
        value_sum[...] = jnp.dot(used_t, value_grad[...], preferred_element_type=F32)

    group, (per, _, width) = query_t.shape[0], out.shape
    share = key_sum.shape[0] // (parts * per)
    slot = 2 * share
    first = lax.rem(me[0] + step, parts) * per
    for i in range(per):
        cols = slice(i * width, (i + 1) * width)
        out[i, :group] = jnp.dot(
            query_t[...], x[0, :, cols], preferred_element_type=F32
        ).astype(BF16)
        out[i, group : 2 * group] = jnp.dot(
            attended_t[...], scaled[0, :, cols], preferred_element_type=F32
        ).astype(BF16)
        here = pl.ds(pl.multiple_of((first + i) * share, 8), share)
        at = 2 * group
        rows = jnp.concatenate([key_sum[here, :], value_sum[here, :]]).astype(BF16)
        for col in range(0, group, width):
            out[i, at : at + slot] = rows[:, col : col + width]
            at += slot


def gradients(me, x_stack, scaled_stack, query_grad, attended, used, key_grad, value_grad, owners):
    parts, rows, width = x_stack.shape
    group = query_grad.shape[1]
    share = parts * width // owners
    per = owners // parts
    enc_width = used.shape[1]
    out_rows = 2 * group + 2 * (enc_width // owners) * group // share
    by_step = pl.BlockSpec((1, rows, width), lambda s, me: (s, 0, 0))
    return pl.pallas_call(
        gradients_kernel,
        out_shape=jax.ShapeDtypeStruct((owners, out_rows, share), BF16),
        grid_spec=pltpu.PrefetchScalarGridSpec(
            num_scalar_prefetch=1,
            grid=(parts,),
            in_specs=[
                by_step, by_step,
                whole(query_grad), whole(attended), whole(used), whole(key_grad), whole(value_grad),
            ],
            out_specs=pl.BlockSpec(
                (per, out_rows, share), lambda s, me: (lax.rem(me[0] + s, parts), 0, 0)
            ),
            scratch_shapes=[
                pltpu.VMEM((group, rows), BF16), pltpu.VMEM((group, rows), BF16),
                pltpu.VMEM((enc_width, group), F32), pltpu.VMEM((enc_width, group), F32),
            ],
        ),
        compiler_params=params(44),
        cost_estimate=cost(8e9, 36 * 2**20),
        name="gradients",
    )(me, x_stack, scaled_stack, query_grad, attended, used, key_grad, value_grad)


def terms_kernel(me, attended, query_grad, wo, wq, *outs):
    step = pl.program_id(0)
    out = jnp.dot(attended[...], wo[...], preferred_element_type=F32).astype(BF16)
    back = contract_cols(query_grad[...], wq[...]).astype(BF16)
    half = out.shape[0] // 2
    for k in (0, 1, 3):

        @pl.when(step == k)
        def _():
            outs[min(k, 2)][0] = out
            outs[min(k, 2)][1] = back

    @pl.when(step == 2)
    def _():
        for i, rows in enumerate((slice(0, half), slice(half, None))):
            outs[3 + i][0] = out[rows]
            outs[3 + i][1] = back[rows]


def model_terms(me, attended, query_grad, wo, wq):
    rows, cols = attended.shape
    width = wo.shape[1] // 4
    ahead = lambda k, me: lax.rem(me[0] + k, 4)
    out = jax.ShapeDtypeStruct((2, rows, width), BF16)
    half = jax.ShapeDtypeStruct((2, rows // 2, width), BF16)
    return pl.pallas_call(
        terms_kernel,
        out_shape=[out] * 3 + [half] * 2,
        grid_spec=pltpu.PrefetchScalarGridSpec(
            num_scalar_prefetch=1,
            grid=(4,),
            in_specs=[
                whole(attended), whole(query_grad),
                pl.BlockSpec((cols, width), lambda k, me: (0, ahead(k, me))),
                pl.BlockSpec((width, cols), lambda k, me: (ahead(k, me), 0)),
            ],
            out_specs=[whole(out)] * 3 + [whole(half)] * 2,
        ),
        compiler_params=params(24),
        cost_estimate=cost(1e6, 2**16),
        name="model_terms",
    )(me, attended, query_grad, wo, wq)


def spread_kernel(where, first, second, third, fourth, kept, given):
    uses = first.shape[0]
    kept[...] = jnp.zeros_like(kept)
    given[...] = jnp.zeros_like(given)
    core, z = where[uses], where[uses + 1]
    chips, enc_dev = kept.shape[0], kept.shape[1]
    total = [summed([t[u] for t in (first, second, third, fourth)]) for u in range(uses)]
    for u in range(uses):
        block = where[u]
        value = total[u]
        for v in range(uses):
            if v != u:
                value = value + jnp.where(where[v] == block, total[v], 0.0)
        value = value.astype(BF16)
        owner = block // enc_dev
        slot = lax.rem(owner // 2 + chips - z, chips)

        @pl.when(lax.rem(owner, 2) == core)
        def _():
            kept[slot, lax.rem(block, enc_dev)] = value

        @pl.when(lax.rem(owner, 2) != core)
        def _():
            given[slot, lax.rem(block, enc_dev)] = value


def spread(where, terms, chips, enc_dev):
    uses, rows, width = terms[0].shape
    out = jax.ShapeDtypeStruct((chips, enc_dev, rows, width), BF16)
    return pl.pallas_call(
        spread_kernel,
        out_shape=(out, out),
        in_specs=[pl.BlockSpec(memory_space=pltpu.SMEM)] + [pl.BlockSpec(memory_space=pltpu.VMEM)] * 4,
        out_specs=(pl.BlockSpec(memory_space=pltpu.VMEM),) * 2,
        compiler_params=params(24),
        cost_estimate=cost(1e11, 2**20),
        name="spread",
    )(where, *terms)


def on_device(x_in, cotangent, tok_weight, neighbours, w_query, w_key, w_value, w_out, encodings):
    x_part = x_in[0]
    cot_part = cotangent[0]
    token_scale = tok_weight[0]
    query_proj = w_query[0]
    key_proj = w_key[0]
    value_proj = w_value[0]
    out_proj = w_out[0]
    enc_local = encodings[0]
    group_cols = query_proj.shape[1]
    enc_dev, enc_rows, enc_width = enc_local.shape
    span_count = neighbours.shape[1]
    use_count = span_count * neighbours.shape[2]
    owners = lax.axis_size("seq")
    chips = owners // 2
    me = lax.axis_index("mp").reshape(1)
    me_seq = lax.axis_index("seq")
    block_ids = neighbours[0].reshape(use_count)

    where = jnp.concatenate([block_ids, jnp.stack([me_seq % 2, me_seq // 2])])
    scaled_part = (token_scale[:, None] * cot_part.astype(F32)).astype(BF16)
    enc_all = lax.all_gather(enc_local, "seq", axis=0, tiled=True)
    x_stack = stacked(gather_mp(x_part))
    scaled_stack = stacked(gather_mp(scaled_part))
    query_rows, attended_grad = project(me, x_stack, scaled_stack, query_proj, out_proj)

    named, query_rows, attended_grad = lax.optimization_barrier(
        (block_ids, query_rows, attended_grad)
    )
    own_rows = pick(named, enc_all).reshape(use_count * enc_rows, enc_width)
    used_pieces = gather_mp(own_rows)
    attended, query_grad, key_grad, value_grad, used = attend(
        used_pieces, key_proj, value_proj, query_rows, attended_grad,
        span_count, 1.0 / math.sqrt(HD),
    )
    grads = gradients(
        me, x_stack, scaled_stack, query_grad, attended, used, key_grad, value_grad, owners
    )
    grads, attended, query_grad, key_grad, value_grad = lax.optimization_barrier(
        (grads, attended, query_grad, key_grad, value_grad)
    )
    use_terms = use_gradients(key_grad, value_grad, key_proj, value_proj, span_count)
    use_terms = exchanged_mp([t.reshape(use_count, enc_rows, enc_width) for t in use_terms])
    terms = model_terms(me, attended, query_grad, out_proj, query_proj)
    grads = lax.psum_scatter(grads, "seq", scatter_dimension=0, tiled=True)[0]

    use_terms, terms = lax.optimization_barrier((use_terms, tuple(terms)))
    kept, given = spread(where, use_terms, chips, enc_dev)
    own, ahead, behind, far_first, far_second = terms
    right, left = shifted(far_first, "mp", 1), shifted(far_second, "mp", -1)
    here = added(kept, other_core(given)).reshape(chips, enc_dev * enc_rows, enc_width)
    arrived, right, left, ahead, behind = lax.optimization_barrier(
        (scatter_z_first(here), right, left, ahead, behind)
    )
    half = ahead.shape[1] // 2
    ahead = jnp.concatenate([added(ahead[:, :half], right), ahead[:, half:]], axis=1)
    behind = jnp.concatenate([behind[:, :half], added(behind[:, half:], left)], axis=1)
    first, third = shifted(ahead, "mp", 1), shifted(behind, "mp", -1)
    arrived, first, third = lax.optimization_barrier(
        (scatter_z_middle(here, arrived), first, third)
    )
    terms = (own, first, third)
    next_input = shifted(summed([x_part, *[t[0] for t in terms]]).astype(BF16), "section", 1)
    prev_grad = shifted(summed([scaled_part, *[t[1] for t in terms]]).astype(BF16), "section", -1)
    arrived = scatter_z_last(here, arrived)
    grad_enc = summed([here[0], *arrived]).astype(BF16)
    grad_enc = grad_enc.reshape(enc_dev, enc_rows, enc_width)

    grad_query, grad_key, grad_value, grad_out = unpacked(grads, group_cols, enc_width // owners)
    return (
        next_input[None],
        prev_grad[None],
        grad_query[None],
        grad_key[None],
        grad_value[None],
        grad_out[None],
        grad_enc[None],
    )


def solution(mesh):
    placed = (
        P("section", "seq", "mp"),
        P("section", "seq", "mp"),
        P("section", "seq"),
        P("section", "seq", None),
        P("section", None, "mp"),
        P("section", None, "mp"),
        P("section", None, "mp"),
        P("section", "mp", None),
        P("section", "seq", "mp", None),
    )
    return jax.shard_map(
        on_device,
        mesh=mesh,
        in_specs=placed,
        out_specs=(
            P("section", "seq", "mp"),
            P("section", "seq", "mp"),
            P("section", "seq", "mp"),
            P("section", "seq", "mp"),
            P("section", "seq", "mp"),
            P("section", "mp", "seq"),
            P("section", "seq", "mp", None),
        ),
        check_vma=False,
    )
```

```python
import functools
import math

import jax
import jax.numpy as jnp
from jax import lax
from jax.experimental import pallas as pl
from jax.experimental.pallas import tpu as pltpu
from jax.sharding import PartitionSpec as P

HD = 128
NBLEN = 128
F32 = jnp.float32
BF16 = jnp.bfloat16


def shifted(value, axis, steps):
    count = lax.axis_size(axis)
    pairs = [(source, (source + steps) % count) for source in range(count)]
    return lax.ppermute(value, axis, pairs)


def along_z(value, steps):
    count = lax.axis_size("seq")
    pairs = [(source, (source + 2 * steps) % count) for source in range(count)]
    return lax.ppermute(value, "seq", pairs)


def other_core(value):
    count = lax.axis_size("seq")
    return lax.ppermute(value, "seq", [(source, source ^ 1) for source in range(count)])


def contract_rows(first_factor, second_factor):
    return lax.dot_general(
        first_factor, second_factor, (((0,), (0,)), ((), ())), preferred_element_type=F32
    )


def contract_cols(first_factor, second_factor):
    return lax.dot_general(
        first_factor, second_factor, (((1,), (1,)), ((), ())), preferred_element_type=F32
    )


def added(first, second):
    return (first.astype(F32) + second.astype(F32)).astype(BF16)


def gather_mp(part):
    half = part.shape[0] // 2
    behind = shifted(part, "mp", 1)
    ahead = shifted(part, "mp", -1)
    far_first = shifted(behind[:half], "mp", 1)
    far_second = shifted(ahead[half:], "mp", -1)
    return part, ahead, far_first, far_second, behind


def pick_kernel(block_ids, blocks, out, done):
    copies = [
        pltpu.make_async_copy(blocks.at[block_ids[u]], out.at[u], done.at[u])
        for u in range(out.shape[0])
    ]
    for copy in copies:
        copy.start()
    for copy in copies:
        copy.wait()


def pick(block_ids, blocks):
    uses = block_ids.shape[0]
    return pl.pallas_call(
        pick_kernel,
        out_shape=jax.ShapeDtypeStruct((uses, *blocks.shape[1:]), BF16),
        in_specs=[pl.BlockSpec(memory_space=pltpu.SMEM), pl.BlockSpec(memory_space=pltpu.HBM)],
        out_specs=pl.BlockSpec(memory_space=pltpu.VMEM),
        scratch_shapes=[pltpu.SemaphoreType.DMA((uses,))],
        compiler_params=params(4),
        cost_estimate=cost(1e6, 2**20),
        name="pick",
    )(block_ids, in_hbm(blocks))


def stacked(pieces):
    own, ahead, far_first, far_second, behind = pieces
    return jnp.stack([own, ahead, jnp.concatenate([far_first, far_second]), behind])


def exchanged_mp(pieces):
    first = shifted(pieces[1], "mp", 1)
    third = shifted(pieces[3], "mp", -1)
    second = shifted(pieces[2], "mp", 2)
    return pieces[0], first, second, third


def summed(terms):
    return sum(term.astype(F32) for term in terms)


def scatter_z_first(terms):
    half = terms.shape[1] // 2
    return along_z(terms[4, :half], 1), along_z(terms[4, half:], -1)


def scatter_z_middle(terms, arrived):
    right, left = arrived
    half = terms.shape[1] // 2
    right = along_z(jnp.concatenate([added(terms[3, :half], right), terms[3, half:]]), 1)
    left = along_z(jnp.concatenate([terms[5, :half], added(terms[5, half:], left)]), -1)
    return along_z(added(terms[2], right), 1), along_z(added(terms[6], left), -1)


def scatter_z_last(terms, arrived):
    right, left = arrived
    return along_z(added(terms[1], right), 1), along_z(added(terms[7], left), -1)


def unpack_kernel(packed, query, key, value, out):
    group, share = query.shape[1], query.shape[0]
    query[...] = packed[:group].T
    out[...] = packed[group : 2 * group]
    rows = key.shape[0]
    at = 2 * group
    for col in range(0, group, share):
        pair = packed[at : at + 2 * rows].astype(F32)
        key[:, col : col + share] = pair[:rows].astype(BF16)
        value[:, col : col + share] = pair[rows:].astype(BF16)
        at += 2 * rows


def unpacked(packed, group, enc_share):
    share = packed.shape[1]
    out = lambda *shape: jax.ShapeDtypeStruct(shape, BF16)
    in_vmem = pl.BlockSpec(memory_space=pltpu.VMEM)
    return pl.pallas_call(
        unpack_kernel,
        out_shape=(out(share, group), out(enc_share, group), out(enc_share, group), out(group, share)),
        in_specs=[in_vmem],
        out_specs=(in_vmem,) * 4,
        compiler_params=params(8),
        cost_estimate=cost(1e6, 2 * 2**20),
        name="unpack",
    )(in_hbm(packed))


def whole(array):
    rank = len(array.shape)
    return pl.BlockSpec(array.shape, lambda *_: (0,) * rank)


def in_hbm(array):
    return pltpu.with_memory_space_constraint(array, pltpu.HBM)


def params(megabytes):
    return pltpu.CompilerParams(vmem_limit_bytes=megabytes * 2**20)


def cost(flops, moved):
    return pl.CostEstimate(flops=int(flops), bytes_accessed=int(moved), transcendentals=0)


def project_kernel(contract, me, rows, weights, out, total):
    step = pl.program_id(0)

    @pl.when(step == 0)
    def _():
        total[...] = jnp.zeros_like(total)

    total[...] += contract(rows[0], weights[...])

    @pl.when(step == pl.num_programs(0) - 1)
    def _():
        out[...] = total[...].astype(BF16)


def project(me, stack, weights, along_rows, name):
    parts, rows, width = stack.shape
    cols = weights.shape[1] if along_rows else weights.shape[0]
    ahead = lambda k, me: lax.rem(me[0] + k, parts)
    if along_rows:
        contract = functools.partial(jnp.dot, preferred_element_type=F32)
        block = pl.BlockSpec((width, cols), lambda k, me: (ahead(k, me), 0))
    else:
        contract = contract_cols
        block = pl.BlockSpec((cols, width), lambda k, me: (0, ahead(k, me)))
    return pl.pallas_call(
        functools.partial(project_kernel, contract),
        out_shape=pltpu.HBM((rows, cols), BF16),
        grid_spec=pltpu.PrefetchScalarGridSpec(
            num_scalar_prefetch=1,
            grid=(parts,),
            in_specs=[pl.BlockSpec((1, rows, width), lambda k, me: (k, 0, 0)), block],
            out_specs=pl.BlockSpec((rows, cols), lambda k, me: (0, 0)),
            scratch_shapes=[pltpu.VMEM((rows, cols), F32)],
        ),
        compiler_params=params(12),
        cost_estimate=cost(1e6, 2**16),
        name=name,
    )(me, stack, weights)


def attend_kernel(scale, span_rows, own, ahead, far_first, far_second, behind, wk, wv, query, grad,
                  attended, query_grad, key_grad, value_grad, used):
    far = jnp.where(pl.program_id(0) == 0, far_first[...], far_second[...])
    spans = query.shape[0] // span_rows
    part = far.shape[0] // spans
    span_keys = 4 * part
    pieces = (own[...], ahead[...], far, behind[...])
    rows = jnp.concatenate(
        [piece[c * part : (c + 1) * part] for c in range(spans) for piece in pieces], axis=0
    )
    used[...] = rows
    keys = jnp.dot(rows, wk[...], preferred_element_type=F32).astype(BF16)
    values = jnp.dot(rows, wv[...], preferred_element_type=F32).astype(BF16)
    query_all, grad_all = query[...], grad[...]
    for c in range(spans):
        at, key_at = slice(c * span_rows, (c + 1) * span_rows), slice(c * span_keys, (c + 1) * span_keys)
        for head in range(query_all.shape[1] // HD):
            cols = slice(head * HD, (head + 1) * HD)
            q, g = query_all[at, cols], grad_all[at, cols]
            k, v = keys[key_at, cols], values[key_at, cols]
            scores = contract_cols(q, k) * scale
            raised = jnp.exp(scores - jnp.max(scores, axis=-1, keepdims=True))
            weights = raised / jnp.sum(raised, axis=-1, keepdims=True)
            half = weights.astype(BF16)
            attended[at, cols] = jnp.dot(half, v, preferred_element_type=F32).astype(BF16)
            soft_grad = contract_cols(g, v)
            row_term = jnp.sum(soft_grad * weights, axis=-1, keepdims=True)
            score_grad = (weights * (soft_grad - row_term) * scale).astype(BF16)
            query_grad[at, cols] = jnp.dot(score_grad, k, preferred_element_type=F32).astype(BF16)
            key_grad[key_at, cols] = contract_rows(score_grad, q).astype(BF16)
            value_grad[key_at, cols] = contract_rows(half, g).astype(BF16)


def use_terms_kernel(spans, key_grad, value_grad, wk, wv, *outs):
    terms = contract_cols(key_grad[...], wk[...]) + contract_cols(value_grad[...], wv[...])
    terms = terms.astype(BF16)
    part = outs[0].shape[0] // spans
    for c in range(spans):
        for k, out in enumerate(outs):
            start = (4 * c + k) * part
            out[c * part : (c + 1) * part] = terms[start : start + part]


def use_gradients(key_grad, value_grad, wk, wv, spans):
    steps = 2
    rows, cols = key_grad.shape
    width = wk.shape[0]
    by_step = lambda height, breadth: pl.BlockSpec((height, breadth), lambda c: (c, 0))
    return pl.pallas_call(
        functools.partial(use_terms_kernel, spans // steps),
        out_shape=[jax.ShapeDtypeStruct((rows // 4, width), BF16)] * 4,
        grid=(steps,),
        in_specs=[by_step(rows // steps, cols), by_step(rows // steps, cols), whole(wk), whole(wv)],
        out_specs=[by_step(rows // 4 // steps, width)] * 4,
        compiler_params=params(20),
        cost_estimate=cost(1e6, 2**16),
        name="use_gradients",
    )(key_grad, value_grad, in_hbm(wk), in_hbm(wv))


def attend(pieces, wk, wv, query, grad, spans, scale):
    own, far_first = pieces[0], pieces[2]
    steps = 2
    part, width = own.shape[0] // steps, own.shape[1]
    rows, cols = query.shape
    by_step = lambda height, breadth: pl.BlockSpec((height, breadth), lambda c: (c, 0))
    out = lambda *shape: jax.ShapeDtypeStruct(shape, BF16)
    return pl.pallas_call(
        functools.partial(attend_kernel, scale, rows // spans),
        out_shape=(
            out(rows, cols), out(rows, cols),
            out(4 * steps * part, cols), out(4 * steps * part, cols),
            out(4 * steps * part, width),
        ),
        grid=(steps,),
        in_specs=[
            by_step(part, width), by_step(part, width), whole(far_first), whole(far_first),
            by_step(part, width),
            whole(wk), whole(wv),
            by_step(rows // steps, cols), by_step(rows // steps, cols),
        ],
        out_specs=(
            by_step(rows // steps, cols), by_step(rows // steps, cols),
            by_step(4 * part, cols), by_step(4 * part, cols),
            by_step(4 * part, width),
        ),
        compiler_params=params(28),
        cost_estimate=cost(4.2e9, 12 * 2**20),
        name="attend",
    )(*pieces, wk, wv, query, grad)


def gradients_kernel(me, x, scaled, query_grad, attended, used, key_grad, value_grad, out,
                     query_t, attended_t, key_sum, value_sum):
    step, parts = pl.program_id(0), pl.num_programs(0)

    @pl.when(step == 0)
    def _():
        query_t[...] = query_grad[...].T
        attended_t[...] = attended[...].T
        used_t = used[...].T
        key_sum[...] = jnp.dot(used_t, key_grad[...], preferred_element_type=F32)
        value_sum[...] = jnp.dot(used_t, value_grad[...], preferred_element_type=F32)

    group, (per, _, width) = query_t.shape[0], out.shape
    share = key_sum.shape[0] // (parts * per)
    slot = 2 * share
    first = lax.rem(me[0] + step, parts) * per
    for i in range(per):
        cols = slice(i * width, (i + 1) * width)
        out[i, :group] = jnp.dot(
            query_t[...], x[0, :, cols], preferred_element_type=F32
        ).astype(BF16)
        out[i, group : 2 * group] = jnp.dot(
            attended_t[...], scaled[0, :, cols], preferred_element_type=F32
        ).astype(BF16)
        here = pl.ds(pl.multiple_of((first + i) * share, 8), share)
        at = 2 * group
        rows = jnp.concatenate([key_sum[here, :], value_sum[here, :]]).astype(BF16)
        for col in range(0, group, width):
            out[i, at : at + slot] = rows[:, col : col + width]
            at += slot


def gradients(me, x_stack, scaled_stack, query_grad, attended, used, key_grad, value_grad, owners):
    parts, rows, width = x_stack.shape
    group = query_grad.shape[1]
    share = parts * width // owners
    per = owners // parts
    enc_width = used.shape[1]
    out_rows = 2 * group + 2 * (enc_width // owners) * group // share
    by_step = pl.BlockSpec((1, rows, width), lambda s, me: (s, 0, 0))
    return pl.pallas_call(
        gradients_kernel,
        out_shape=pltpu.HBM((owners, out_rows, share), BF16),
        grid_spec=pltpu.PrefetchScalarGridSpec(
            num_scalar_prefetch=1,
            grid=(parts,),
            in_specs=[
                by_step, by_step,
                whole(query_grad), whole(attended), whole(used), whole(key_grad), whole(value_grad),
            ],
            out_specs=pl.BlockSpec(
                (per, out_rows, share), lambda s, me: (lax.rem(me[0] + s, parts), 0, 0)
            ),
            scratch_shapes=[
                pltpu.VMEM((group, rows), BF16), pltpu.VMEM((group, rows), BF16),
                pltpu.VMEM((enc_width, group), F32), pltpu.VMEM((enc_width, group), F32),
            ],
        ),
        compiler_params=params(28),
        cost_estimate=cost(8e9, 36 * 2**20),
        name="gradients",
    )(me, x_stack, scaled_stack, query_grad, attended, used, key_grad, value_grad)


def terms_kernel(me, attended, query_grad, wo, wq, *outs):
    step = pl.program_id(0)
    out = jnp.dot(attended[...], wo[...], preferred_element_type=F32).astype(BF16)
    back = contract_cols(query_grad[...], wq[...]).astype(BF16)
    half = out.shape[0] // 2
    for k in (0, 1, 3):

        @pl.when(step == k)
        def _():
            outs[min(k, 2)][0] = out
            outs[min(k, 2)][1] = back

    @pl.when(step == 2)
    def _():
        for i, rows in enumerate((slice(0, half), slice(half, None))):
            outs[3 + i][0] = out[rows]
            outs[3 + i][1] = back[rows]


def model_terms(me, attended, query_grad, wo, wq):
    rows, cols = attended.shape
    width = wo.shape[1] // 4
    ahead = lambda k, me: lax.rem(me[0] + k, 4)
    out = jax.ShapeDtypeStruct((2, rows, width), BF16)
    half = jax.ShapeDtypeStruct((2, rows // 2, width), BF16)
    return pl.pallas_call(
        terms_kernel,
        out_shape=[out] * 3 + [half] * 2,
        grid_spec=pltpu.PrefetchScalarGridSpec(
            num_scalar_prefetch=1,
            grid=(4,),
            in_specs=[
                whole(attended), whole(query_grad),
                pl.BlockSpec((cols, width), lambda k, me: (0, ahead(k, me))),
                pl.BlockSpec((width, cols), lambda k, me: (ahead(k, me), 0)),
            ],
            out_specs=[whole(out)] * 3 + [whole(half)] * 2,
        ),
        compiler_params=params(24),
        cost_estimate=cost(1e6, 2**16),
        name="model_terms",
    )(me, attended, query_grad, wo, wq)


def spread_kernel(where, first, second, third, fourth, kept, given):
    uses = first.shape[0]
    kept[...] = jnp.zeros_like(kept)
    given[...] = jnp.zeros_like(given)
    core, z = where[uses], where[uses + 1]
    chips, enc_dev = kept.shape[0], kept.shape[1]
    total = [summed([t[u] for t in (first, second, third, fourth)]) for u in range(uses)]
    for u in range(uses):
        block = where[u]
        value = total[u]
        for v in range(uses):
            if v != u:
                value = value + jnp.where(where[v] == block, total[v], 0.0)
        value = value.astype(BF16)
        owner = block // enc_dev
        slot = lax.rem(owner // 2 + chips - z, chips)

        @pl.when(lax.rem(owner, 2) == core)
        def _():
            kept[slot, lax.rem(block, enc_dev)] = value

        @pl.when(lax.rem(owner, 2) != core)
        def _():
            given[slot, lax.rem(block, enc_dev)] = value


def spread(where, terms, chips, enc_dev):
    uses, rows, width = terms[0].shape
    out = jax.ShapeDtypeStruct((chips, enc_dev, rows, width), BF16)
    return pl.pallas_call(
        spread_kernel,
        out_shape=(out, out),
        in_specs=[pl.BlockSpec(memory_space=pltpu.SMEM)] + [pl.BlockSpec(memory_space=pltpu.VMEM)] * 4,
        out_specs=(pl.BlockSpec(memory_space=pltpu.VMEM),) * 2,
        compiler_params=params(24),
        cost_estimate=cost(1e11, 2**20),
        name="spread",
    )(where, *terms)


def on_device(x_in, cotangent, tok_weight, neighbours, w_query, w_key, w_value, w_out, encodings):
    x_part = x_in[0]
    cot_part = cotangent[0]
    token_scale = tok_weight[0]
    query_proj = w_query[0]
    key_proj = w_key[0]
    value_proj = w_value[0]
    out_proj = w_out[0]
    enc_local = encodings[0]
    group_cols = query_proj.shape[1]
    enc_dev, enc_rows, enc_width = enc_local.shape
    span_count = neighbours.shape[1]
    use_count = span_count * neighbours.shape[2]
    owners = lax.axis_size("seq")
    chips = owners // 2
    me = lax.axis_index("mp").reshape(1)
    me_seq = lax.axis_index("seq")
    block_ids = neighbours[0].reshape(use_count)

    where = jnp.concatenate([block_ids, jnp.stack([me_seq % 2, me_seq // 2])])
    scaled_part = (token_scale[:, None] * cot_part.astype(F32)).astype(BF16)
    enc_all = lax.all_gather(enc_local, "seq", axis=0, tiled=True)
    x_stack = stacked(gather_mp(x_part))
    scaled_stack = stacked(gather_mp(scaled_part))
    query_rows = project(me, x_stack, query_proj, True, "project_query")
    attended_grad = project(me, scaled_stack, out_proj, False, "project_grad")

    named, query_rows, attended_grad = lax.optimization_barrier(
        (block_ids, query_rows, attended_grad)
    )
    own_rows = pick(named, enc_all).reshape(use_count * enc_rows, enc_width)
    used_pieces = gather_mp(own_rows)
    attended, query_grad, key_grad, value_grad, used = attend(
        used_pieces, key_proj, value_proj, query_rows, attended_grad,
        span_count, 1.0 / math.sqrt(HD),
    )
    grads = gradients(
        me, x_stack, scaled_stack, query_grad, attended, used, key_grad, value_grad, owners
    )
    grads, attended, query_grad, key_grad, value_grad = lax.optimization_barrier(
        (grads, attended, query_grad, key_grad, value_grad)
    )
    use_terms = use_gradients(key_grad, value_grad, key_proj, value_proj, span_count)
    use_terms = exchanged_mp([t.reshape(use_count, enc_rows, enc_width) for t in use_terms])
    terms = model_terms(me, attended, query_grad, out_proj, query_proj)
    grads = lax.psum_scatter(grads, "seq", scatter_dimension=0, tiled=True)[0]

    use_terms, terms = lax.optimization_barrier((use_terms, tuple(terms)))
    kept, given = spread(where, use_terms, chips, enc_dev)
    own, ahead, behind, far_first, far_second = terms
    right, left = shifted(far_first, "mp", 1), shifted(far_second, "mp", -1)
    here = added(kept, other_core(given)).reshape(chips, enc_dev * enc_rows, enc_width)
    arrived, right, left, ahead, behind = lax.optimization_barrier(
        (scatter_z_first(here), right, left, ahead, behind)
    )
    half = ahead.shape[1] // 2
    ahead = jnp.concatenate([added(ahead[:, :half], right), ahead[:, half:]], axis=1)
    behind = jnp.concatenate([behind[:, :half], added(behind[:, half:], left)], axis=1)
    first, third = shifted(ahead, "mp", 1), shifted(behind, "mp", -1)
    arrived, first, third = lax.optimization_barrier(
        (scatter_z_middle(here, arrived), first, third)
    )
    terms = (own, first, third)
    next_input = shifted(summed([x_part, *[t[0] for t in terms]]).astype(BF16), "section", 1)
    prev_grad = shifted(summed([scaled_part, *[t[1] for t in terms]]).astype(BF16), "section", -1)
    arrived = scatter_z_last(here, arrived)
    grad_enc = summed([here[0], *arrived]).astype(BF16)
    grad_enc = grad_enc.reshape(enc_dev, enc_rows, enc_width)

    grad_query, grad_key, grad_value, grad_out = unpacked(grads, group_cols, enc_width // owners)
    return (
        next_input[None],
        prev_grad[None],
        grad_query[None],
        grad_key[None],
        grad_value[None],
        grad_out[None],
        grad_enc[None],
    )


def solution(mesh):
    placed = (
        P("section", "seq", "mp"),
        P("section", "seq", "mp"),
        P("section", "seq"),
        P("section", "seq", None),
        P("section", None, "mp"),
        P("section", None, "mp"),
        P("section", None, "mp"),
        P("section", "mp", None),
        P("section", "seq", "mp", None),
    )
    return jax.shard_map(
        on_device,
        mesh=mesh,
        in_specs=placed,
        out_specs=(
            P("section", "seq", "mp"),
            P("section", "seq", "mp"),
            P("section", "seq", "mp"),
            P("section", "seq", "mp"),
            P("section", "seq", "mp"),
            P("section", "mp", "seq"),
            P("section", "seq", "mp", None),
        ),
        check_vma=False,
    )
```

```python
import functools
import math

import jax
import jax.numpy as jnp
from jax import lax
from jax.experimental import pallas as pl
from jax.experimental.pallas import tpu as pltpu
from jax.sharding import PartitionSpec as P

HD = 128
NBLEN = 128
F32 = jnp.float32
BF16 = jnp.bfloat16


def shifted(value, axis, steps):
    count = lax.axis_size(axis)
    pairs = [(source, (source + steps) % count) for source in range(count)]
    return lax.ppermute(value, axis, pairs)


def along_z(value, steps):
    count = lax.axis_size("seq")
    pairs = [(source, (source + 2 * steps) % count) for source in range(count)]
    return lax.ppermute(value, "seq", pairs)


def other_core(value):
    count = lax.axis_size("seq")
    return lax.ppermute(value, "seq", [(source, source ^ 1) for source in range(count)])


def contract_rows(first_factor, second_factor):
    return lax.dot_general(
        first_factor, second_factor, (((0,), (0,)), ((), ())), preferred_element_type=F32
    )


def contract_cols(first_factor, second_factor):
    return lax.dot_general(
        first_factor, second_factor, (((1,), (1,)), ((), ())), preferred_element_type=F32
    )


def added(first, second):
    return (first.astype(F32) + second.astype(F32)).astype(BF16)


def gather_mp(part):
    half = part.shape[0] // 2
    behind = shifted(part, "mp", 1)
    ahead = shifted(part, "mp", -1)
    far_first = shifted(behind[:half], "mp", 1)
    far_second = shifted(ahead[half:], "mp", -1)
    return part, ahead, far_first, far_second, behind


def pick_kernel(block_ids, blocks, out, done):
    copies = [
        pltpu.make_async_copy(blocks.at[block_ids[u]], out.at[u], done.at[u])
        for u in range(out.shape[0])
    ]
    for copy in copies:
        copy.start()
    for copy in copies:
        copy.wait()


def pick(block_ids, blocks):
    uses = block_ids.shape[0]
    return pl.pallas_call(
        pick_kernel,
        out_shape=jax.ShapeDtypeStruct((uses, *blocks.shape[1:]), BF16),
        in_specs=[pl.BlockSpec(memory_space=pltpu.SMEM), pl.BlockSpec(memory_space=pltpu.HBM)],
        out_specs=pl.BlockSpec(memory_space=pltpu.VMEM),
        scratch_shapes=[pltpu.SemaphoreType.DMA((uses,))],
        compiler_params=params(4),
        cost_estimate=cost(1e6, 2**20),
        name="pick",
    )(block_ids, in_hbm(blocks))


def stacked(pieces):
    own, ahead, far_first, far_second, behind = pieces
    return jnp.stack([own, ahead, jnp.concatenate([far_first, far_second]), behind])


def exchanged_mp(pieces):
    first = shifted(pieces[1], "mp", 1)
    third = shifted(pieces[3], "mp", -1)
    second = shifted(pieces[2], "mp", 2)
    return pieces[0], first, second, third


def summed(terms):
    return sum(term.astype(F32) for term in terms)


def scatter_z_first(terms):
    half = terms.shape[1] // 2
    return along_z(terms[4, :half], 1), along_z(terms[4, half:], -1)


def scatter_z_middle(terms, arrived):
    right, left = arrived
    half = terms.shape[1] // 2
    right = along_z(jnp.concatenate([added(terms[3, :half], right), terms[3, half:]]), 1)
    left = along_z(jnp.concatenate([terms[5, :half], added(terms[5, half:], left)]), -1)
    return along_z(added(terms[2], right), 1), along_z(added(terms[6], left), -1)


def scatter_z_last(terms, arrived):
    right, left = arrived
    return along_z(added(terms[1], right), 1), along_z(added(terms[7], left), -1)


def unpack_kernel(packed, query, key, value, out):
    group, share = query.shape[1], query.shape[0]
    query[...] = packed[:group].T
    out[...] = packed[group : 2 * group]
    rows = key.shape[0]
    at = 2 * group
    for col in range(0, group, share):
        pair = packed[at : at + 2 * rows].astype(F32)
        key[:, col : col + share] = pair[:rows].astype(BF16)
        value[:, col : col + share] = pair[rows:].astype(BF16)
        at += 2 * rows


def unpacked(packed, group, enc_share):
    share = packed.shape[1]
    out = lambda *shape: jax.ShapeDtypeStruct(shape, BF16)
    in_vmem = pl.BlockSpec(memory_space=pltpu.VMEM)
    return pl.pallas_call(
        unpack_kernel,
        out_shape=(out(share, group), out(enc_share, group), out(enc_share, group), out(group, share)),
        in_specs=[in_vmem],
        out_specs=(in_vmem,) * 4,
        compiler_params=params(8),
        cost_estimate=cost(1e6, 2 * 2**20),
        name="unpack",
    )(in_hbm(packed))


def whole(array):
    rank = len(array.shape)
    return pl.BlockSpec(array.shape, lambda *_: (0,) * rank)


def in_hbm(array):
    return pltpu.with_memory_space_constraint(array, pltpu.HBM)


def params(megabytes):
    return pltpu.CompilerParams(vmem_limit_bytes=megabytes * 2**20)


def cost(flops, moved):
    return pl.CostEstimate(flops=int(flops), bytes_accessed=int(moved), transcendentals=0)


def project_kernel(contract, me, rows, weights, out, total):
    step = pl.program_id(0)

    @pl.when(step == 0)
    def _():
        total[...] = jnp.zeros_like(total)

    total[...] += contract(rows[0], weights[...])

    @pl.when(step == pl.num_programs(0) - 1)
    def _():
        out[...] = total[...].astype(BF16)


def project(me, stack, weights, along_rows, name):
    parts, rows, width = stack.shape
    cols = weights.shape[1] if along_rows else weights.shape[0]
    ahead = lambda k, me: lax.rem(me[0] + k, parts)
    if along_rows:
        contract = functools.partial(jnp.dot, preferred_element_type=F32)
        block = pl.BlockSpec((width, cols), lambda k, me: (ahead(k, me), 0))
    else:
        contract = contract_cols
        block = pl.BlockSpec((cols, width), lambda k, me: (0, ahead(k, me)))
    return pl.pallas_call(
        functools.partial(project_kernel, contract),
        out_shape=pltpu.HBM((rows, cols), BF16),
        grid_spec=pltpu.PrefetchScalarGridSpec(
            num_scalar_prefetch=1,
            grid=(parts,),
            in_specs=[pl.BlockSpec((1, rows, width), lambda k, me: (k, 0, 0)), block],
            out_specs=pl.BlockSpec((rows, cols), lambda k, me: (0, 0)),
            scratch_shapes=[pltpu.VMEM((rows, cols), F32)],
        ),
        compiler_params=params(8),
        cost_estimate=cost(1e6, 2**16),
        name=name,
    )(me, stack, weights)


def attend_kernel(scale, span_rows, own, ahead, far_first, far_second, behind, wk, wv, query, grad,
                  attended, query_grad, key_grad, value_grad, used):
    far = jnp.where(pl.program_id(0) == 0, far_first[...], far_second[...])
    spans = query.shape[0] // span_rows
    part = far.shape[0] // spans
    span_keys = 4 * part
    pieces = (own[...], ahead[...], far, behind[...])
    rows = jnp.concatenate(
        [piece[c * part : (c + 1) * part] for c in range(spans) for piece in pieces], axis=0
    )
    used[...] = rows
    keys = jnp.dot(rows, wk[...], preferred_element_type=F32).astype(BF16)
    values = jnp.dot(rows, wv[...], preferred_element_type=F32).astype(BF16)
    query_all, grad_all = query[...], grad[...]
    for c in range(spans):
        at, key_at = slice(c * span_rows, (c + 1) * span_rows), slice(c * span_keys, (c + 1) * span_keys)
        for head in range(query_all.shape[1] // HD):
            cols = slice(head * HD, (head + 1) * HD)
            q, g = query_all[at, cols], grad_all[at, cols]
            k, v = keys[key_at, cols], values[key_at, cols]
            scores = contract_cols(q, k) * scale
            raised = jnp.exp(scores - jnp.max(scores, axis=-1, keepdims=True))
            weights = raised / jnp.sum(raised, axis=-1, keepdims=True)
            half = weights.astype(BF16)
            attended[at, cols] = jnp.dot(half, v, preferred_element_type=F32).astype(BF16)
            soft_grad = contract_cols(g, v)
            row_term = jnp.sum(soft_grad * weights, axis=-1, keepdims=True)
            score_grad = (weights * (soft_grad - row_term) * scale).astype(BF16)
            query_grad[at, cols] = jnp.dot(score_grad, k, preferred_element_type=F32).astype(BF16)
            key_grad[key_at, cols] = contract_rows(score_grad, q).astype(BF16)
            value_grad[key_at, cols] = contract_rows(half, g).astype(BF16)


def use_terms_kernel(spans, key_grad, value_grad, wk, wv, *outs):
    terms = contract_cols(key_grad[...], wk[...]) + contract_cols(value_grad[...], wv[...])
    terms = terms.astype(BF16)
    part = outs[0].shape[0] // spans
    for c in range(spans):
        for k, out in enumerate(outs):
            start = (4 * c + k) * part
            out[c * part : (c + 1) * part] = terms[start : start + part]


def use_gradients(key_grad, value_grad, wk, wv, spans):
    steps = 2
    rows, cols = key_grad.shape
    width = wk.shape[0]
    by_step = lambda height, breadth: pl.BlockSpec((height, breadth), lambda c: (c, 0))
    return pl.pallas_call(
        functools.partial(use_terms_kernel, spans // steps),
        out_shape=[jax.ShapeDtypeStruct((rows // 4, width), BF16)] * 4,
        grid=(steps,),
        in_specs=[by_step(rows // steps, cols), by_step(rows // steps, cols), whole(wk), whole(wv)],
        out_specs=[by_step(rows // 4 // steps, width)] * 4,
        compiler_params=params(14),
        cost_estimate=cost(1e6, 2**16),
        name="use_gradients",
    )(in_hbm(key_grad), in_hbm(value_grad), in_hbm(wk), in_hbm(wv))


def attend(pieces, wk, wv, query, grad, spans, scale):
    own, far_first = pieces[0], pieces[2]
    steps = 2
    part, width = own.shape[0] // steps, own.shape[1]
    rows, cols = query.shape
    by_step = lambda height, breadth: pl.BlockSpec((height, breadth), lambda c: (c, 0))
    out = lambda *shape: jax.ShapeDtypeStruct(shape, BF16)
    return pl.pallas_call(
        functools.partial(attend_kernel, scale, rows // spans),
        out_shape=(
            out(rows, cols), out(rows, cols),
            out(4 * steps * part, cols), out(4 * steps * part, cols),
            out(4 * steps * part, width),
        ),
        grid=(steps,),
        in_specs=[
            by_step(part, width), by_step(part, width), whole(far_first), whole(far_first),
            by_step(part, width),
            whole(wk), whole(wv),
            by_step(rows // steps, cols), by_step(rows // steps, cols),
        ],
        out_specs=(
            by_step(rows // steps, cols), by_step(rows // steps, cols),
            by_step(4 * part, cols), by_step(4 * part, cols),
            by_step(4 * part, width),
        ),
        compiler_params=params(18),
        cost_estimate=cost(4.2e9, 12 * 2**20),
        name="attend",
    )(*pieces, wk, wv, query, grad)


def gradients_kernel(me, x, scaled, query_grad, attended, used, key_grad, value_grad, out,
                     query_t, attended_t, key_sum, value_sum):
    step, parts = pl.program_id(0), pl.num_programs(0)

    @pl.when(step == 0)
    def _():
        query_t[...] = query_grad[...].T
        attended_t[...] = attended[...].T
        used_t = used[...].T
        key_sum[...] = jnp.dot(used_t, key_grad[...], preferred_element_type=F32)
        value_sum[...] = jnp.dot(used_t, value_grad[...], preferred_element_type=F32)

    group, (per, _, width) = query_t.shape[0], out.shape
    share = key_sum.shape[0] // (parts * per)
    slot = 2 * share
    first = lax.rem(me[0] + step, parts) * per
    for i in range(per):
        cols = slice(i * width, (i + 1) * width)
        out[i, :group] = jnp.dot(
            query_t[...], x[0, :, cols], preferred_element_type=F32
        ).astype(BF16)
        out[i, group : 2 * group] = jnp.dot(
            attended_t[...], scaled[0, :, cols], preferred_element_type=F32
        ).astype(BF16)
        here = pl.ds(pl.multiple_of((first + i) * share, 8), share)
        at = 2 * group
        rows = jnp.concatenate([key_sum[here, :], value_sum[here, :]]).astype(BF16)
        for col in range(0, group, width):
            out[i, at : at + slot] = rows[:, col : col + width]
            at += slot


def gradients(me, x_stack, scaled_stack, query_grad, attended, used, key_grad, value_grad, owners):
    parts, rows, width = x_stack.shape
    group = query_grad.shape[1]
    share = parts * width // owners
    per = owners // parts
    enc_width = used.shape[1]
    out_rows = 2 * group + 2 * (enc_width // owners) * group // share
    by_step = pl.BlockSpec((1, rows, width), lambda s, me: (s, 0, 0))
    return pl.pallas_call(
        gradients_kernel,
        out_shape=pltpu.HBM((owners, out_rows, share), BF16),
        grid_spec=pltpu.PrefetchScalarGridSpec(
            num_scalar_prefetch=1,
            grid=(parts,),
            in_specs=[
                by_step, by_step,
                whole(query_grad), whole(attended), whole(used), whole(key_grad), whole(value_grad),
            ],
            out_specs=pl.BlockSpec(
                (per, out_rows, share), lambda s, me: (lax.rem(me[0] + s, parts), 0, 0)
            ),
            scratch_shapes=[
                pltpu.VMEM((group, rows), BF16), pltpu.VMEM((group, rows), BF16),
                pltpu.VMEM((enc_width, group), F32), pltpu.VMEM((enc_width, group), F32),
            ],
        ),
        compiler_params=params(28),
        cost_estimate=cost(8e9, 36 * 2**20),
        name="gradients",
    )(me, x_stack, scaled_stack, query_grad, attended, used, key_grad, value_grad)


def terms_kernel(me, attended, query_grad, wo, wq, *outs):
    step = pl.program_id(0)
    out = jnp.dot(attended[...], wo[...], preferred_element_type=F32).astype(BF16)
    back = contract_cols(query_grad[...], wq[...]).astype(BF16)
    half = out.shape[0] // 2
    for k in (0, 1, 3):

        @pl.when(step == k)
        def _():
            outs[min(k, 2)][0] = out
            outs[min(k, 2)][1] = back

    @pl.when(step == 2)
    def _():
        for i, rows in enumerate((slice(0, half), slice(half, None))):
            outs[3 + i][0] = out[rows]
            outs[3 + i][1] = back[rows]


def model_terms(me, attended, query_grad, wo, wq):
    rows, cols = attended.shape
    width = wo.shape[1] // 4
    ahead = lambda k, me: lax.rem(me[0] + k, 4)
    out = jax.ShapeDtypeStruct((2, rows, width), BF16)
    half = jax.ShapeDtypeStruct((2, rows // 2, width), BF16)
    return pl.pallas_call(
        terms_kernel,
        out_shape=[out] * 3 + [half] * 2,
        grid_spec=pltpu.PrefetchScalarGridSpec(
            num_scalar_prefetch=1,
            grid=(4,),
            in_specs=[
                whole(attended), whole(query_grad),
                pl.BlockSpec((cols, width), lambda k, me: (0, ahead(k, me))),
                pl.BlockSpec((width, cols), lambda k, me: (ahead(k, me), 0)),
            ],
            out_specs=[whole(out)] * 3 + [whole(half)] * 2,
        ),
        compiler_params=params(24),
        cost_estimate=cost(1e6, 2**16),
        name="model_terms",
    )(me, attended, query_grad, wo, wq)


def spread_kernel(where, first, second, third, fourth, kept, given):
    uses = first.shape[0]
    kept[...] = jnp.zeros_like(kept)
    given[...] = jnp.zeros_like(given)
    core, z = where[uses], where[uses + 1]
    chips, enc_dev = kept.shape[0], kept.shape[1]
    total = [summed([t[u] for t in (first, second, third, fourth)]) for u in range(uses)]
    for u in range(uses):
        block = where[u]
        value = total[u]
        for v in range(uses):
            if v != u:
                value = value + jnp.where(where[v] == block, total[v], 0.0)
        value = value.astype(BF16)
        owner = block // enc_dev
        slot = lax.rem(owner // 2 + chips - z, chips)

        @pl.when(lax.rem(owner, 2) == core)
        def _():
            kept[slot, lax.rem(block, enc_dev)] = value

        @pl.when(lax.rem(owner, 2) != core)
        def _():
            given[slot, lax.rem(block, enc_dev)] = value


def spread(where, terms, chips, enc_dev):
    uses, rows, width = terms[0].shape
    out = jax.ShapeDtypeStruct((chips, enc_dev, rows, width), BF16)
    return pl.pallas_call(
        spread_kernel,
        out_shape=(out, out),
        in_specs=[pl.BlockSpec(memory_space=pltpu.SMEM)] + [pl.BlockSpec(memory_space=pltpu.VMEM)] * 4,
        out_specs=(pl.BlockSpec(memory_space=pltpu.VMEM),) * 2,
        compiler_params=params(24),
        cost_estimate=cost(1e11, 2**20),
        name="spread",
    )(where, *terms)


def on_device(x_in, cotangent, tok_weight, neighbours, w_query, w_key, w_value, w_out, encodings):
    x_part = x_in[0]
    cot_part = cotangent[0]
    token_scale = tok_weight[0]
    query_proj = w_query[0]
    key_proj = w_key[0]
    value_proj = w_value[0]
    out_proj = w_out[0]
    enc_local = encodings[0]
    group_cols = query_proj.shape[1]
    enc_dev, enc_rows, enc_width = enc_local.shape
    span_count = neighbours.shape[1]
    use_count = span_count * neighbours.shape[2]
    owners = lax.axis_size("seq")
    chips = owners // 2
    me = lax.axis_index("mp").reshape(1)
    me_seq = lax.axis_index("seq")
    block_ids = neighbours[0].reshape(use_count)

    where = jnp.concatenate([block_ids, jnp.stack([me_seq % 2, me_seq // 2])])
    scaled_part = (token_scale[:, None] * cot_part.astype(F32)).astype(BF16)
    enc_all = lax.all_gather(enc_local, "seq", axis=0, tiled=True)
    x_stack = stacked(gather_mp(x_part))
    scaled_stack = stacked(gather_mp(scaled_part))
    query_rows = project(me, x_stack, query_proj, True, "project_query")
    attended_grad = project(me, scaled_stack, out_proj, False, "project_grad")

    named, query_rows, attended_grad = lax.optimization_barrier(
        (block_ids, query_rows, attended_grad)
    )
    own_rows = pick(named, enc_all).reshape(use_count * enc_rows, enc_width)
    used_pieces = gather_mp(own_rows)
    attended, query_grad, key_grad, value_grad, used = attend(
        used_pieces, key_proj, value_proj, query_rows, attended_grad,
        span_count, 1.0 / math.sqrt(HD),
    )
    grads = gradients(
        me, x_stack, scaled_stack, query_grad, attended, used, key_grad, value_grad, owners
    )
    grads, attended, query_grad, key_grad, value_grad = lax.optimization_barrier(
        (grads, attended, query_grad, key_grad, value_grad)
    )
    use_terms = use_gradients(key_grad, value_grad, key_proj, value_proj, span_count)
    use_terms = exchanged_mp([t.reshape(use_count, enc_rows, enc_width) for t in use_terms])
    terms = model_terms(me, attended, query_grad, out_proj, query_proj)
    grads = lax.psum_scatter(grads, "seq", scatter_dimension=0, tiled=True)[0]

    use_terms, terms = lax.optimization_barrier((use_terms, tuple(terms)))
    kept, given = spread(where, use_terms, chips, enc_dev)
    own, ahead, behind, far_first, far_second = terms
    right, left = shifted(far_first, "mp", 1), shifted(far_second, "mp", -1)
    here = added(kept, other_core(given)).reshape(chips, enc_dev * enc_rows, enc_width)
    arrived, right, left, ahead, behind = lax.optimization_barrier(
        (scatter_z_first(here), right, left, ahead, behind)
    )
    half = ahead.shape[1] // 2
    ahead = jnp.concatenate([added(ahead[:, :half], right), ahead[:, half:]], axis=1)
    behind = jnp.concatenate([behind[:, :half], added(behind[:, half:], left)], axis=1)
    first, third = shifted(ahead, "mp", 1), shifted(behind, "mp", -1)
    arrived, first, third = lax.optimization_barrier(
        (scatter_z_middle(here, arrived), first, third)
    )
    terms = (own, first, third)
    next_input = shifted(summed([x_part, *[t[0] for t in terms]]).astype(BF16), "section", 1)
    prev_grad = shifted(summed([scaled_part, *[t[1] for t in terms]]).astype(BF16), "section", -1)
    arrived = scatter_z_last(here, arrived)
    grad_enc = summed([here[0], *arrived]).astype(BF16)
    grad_enc = grad_enc.reshape(enc_dev, enc_rows, enc_width)

    grad_query, grad_key, grad_value, grad_out = unpacked(grads, group_cols, enc_width // owners)
    return (
        next_input[None],
        prev_grad[None],
        grad_query[None],
        grad_key[None],
        grad_value[None],
        grad_out[None],
        grad_enc[None],
    )


def solution(mesh):
    placed = (
        P("section", "seq", "mp"),
        P("section", "seq", "mp"),
        P("section", "seq"),
        P("section", "seq", None),
        P("section", None, "mp"),
        P("section", None, "mp"),
        P("section", None, "mp"),
        P("section", "mp", None),
        P("section", "seq", "mp", None),
    )
    return jax.shard_map(
        on_device,
        mesh=mesh,
        in_specs=placed,
        out_specs=(
            P("section", "seq", "mp"),
            P("section", "seq", "mp"),
            P("section", "seq", "mp"),
            P("section", "seq", "mp"),
            P("section", "seq", "mp"),
            P("section", "mp", "seq"),
            P("section", "seq", "mp", None),
        ),
        check_vma=False,
    )
```
